32 devices in a mesh: dp: 8 (over z, x), fsdp: 4 (over y, core).
Axes of the slice: x: 2, y: 2, z: 4, core: 2. Of those that a mesh axis runs over, the one named last changes fastest.
Arguments:
- tokens: bfloat16 [3, 12288, 576], P(None, ('dp', 'fsdp')), may hold values from -6 to 6
- cotangent: bfloat16 [3, 12288, 576], P(None, ('dp', 'fsdp')), may hold values from -6 to 6
- lengths: int32 [3, 8, 3], P(None, 'dp'), may hold values from 0 to 1536, as said below
- gain_attn: bfloat16 [576], P('dp'), may hold values from 0.099609375 to 1.8984375
- w_query: bfloat16 [576, 576], P('dp', 'fsdp'), may hold values from -0.25 to 0.25
- w_key: bfloat16 [576, 192], P('dp', 'fsdp'), may hold values from -0.25 to 0.25
- w_value: bfloat16 [576, 192], P('dp', 'fsdp'), may hold values from -0.25 to 0.25
- w_out: bfloat16 [576, 576], P('dp', 'fsdp'), may hold values from -2 to 2
- gain_mlp: bfloat16 [576], P('dp'), may hold values from 0.099609375 to 1.8984375
- w_gate: bfloat16 [576, 1536], P('dp', 'fsdp'), may hold values from -0.25 to 0.25
- w_up: bfloat16 [576, 1536], P('dp', 'fsdp'), may hold values from -0.25 to 0.25
- w_down: bfloat16 [1536, 576], P('dp', 'fsdp'), may hold values from -0.15625 to 0.15625
Outputs:
- mixed: bfloat16 [3, 12288, 576], P(None, ('dp', 'fsdp'))
- input_grad: float32 [3, 12288, 576], P(None, ('dp', 'fsdp'))
- grad_gain_attn: float32 [576], P('dp')
- grad_query: float32 [576, 576], P('dp', 'fsdp')
- grad_key: float32 [576, 192], P('dp', 'fsdp')
- grad_value: float32 [576, 192], P('dp', 'fsdp')
- grad_out: float32 [576, 576], P('dp', 'fsdp')
- grad_gain_mlp: float32 [576], P('dp')
- grad_gate: float32 [576, 1536], P('dp', 'fsdp')
- grad_up: float32 [576, 1536], P('dp', 'fsdp')
- grad_down: float32 [1536, 576], P('dp', 'fsdp')
The draws below stay inside these ranges and needn't reach their ends.
Inputs may be any that keep to these rules, and one draw needn't show every extreme that they name: lengths[m, g] lists in order the lengths of the 3 sequences (some may be empty) packed from the first token of group g of micro-batch m; they sum to at most 1536, the tokens after them being padding, and one of them is 1153 or longer.
All inputs are finite; a program needn't handle non-finite values.
Results may differ from the reference program's by a relative error of at most 0.017.
Values may be sent and summed in bfloat16 or wider, within the bound.
No kernel may reach another device: no remote copies, remote signals or barrier semaphores. Data moves between devices by JAX's collectives and lax.ppermute only.
A program may use at most 320 MiB of HBM per device.

```python
import math
import jax
import jax.numpy as jnp
from jax import lax

D = 576
HEADS = 9
KV_HEADS = 3
HEAD_DIM = 64
FF = 1536
MICRO = 3
SEQS = 3
GROUPS = 8
GROUP_TOK = 1536
LONG_MIN = 1153
TOKENS_MB = 12288


def draw_lengths(key, part):
    key = jax.random.fold_in(key, 11)
    subkeys = jax.random.split(key, 5)
    grid_shape = (MICRO, GROUPS)
    longest = jax.random.randint(subkeys[0], grid_shape, LONG_MIN, GROUP_TOK + 1)
    full_group = jax.random.randint(subkeys[1], (MICRO, 1), 0, GROUPS)
    column = jnp.arange(GROUPS, dtype=jnp.int32)[None, :]
    longest = jnp.where(column == full_group, GROUP_TOK, longest)
    spare_room = GROUP_TOK - longest
    extra_total = jax.random.randint(subkeys[2], grid_shape, 0, 1 << 20) % (spare_room + 1)
    first_cut = jax.random.randint(subkeys[3], grid_shape, 0, 1 << 20) % (extra_total + 1)
    second_cut = extra_total - first_cut
    long_slot = jax.random.randint(subkeys[4], grid_shape, 0, 3)
    column_zero = jnp.where(long_slot == 0, longest, first_cut)
    column_one = jnp.where(long_slot == 1, longest, jnp.where(long_slot == 0, first_cut, second_cut))
    column_two = jnp.where(long_slot == 2, longest, second_cut)
    return jnp.stack([column_zero, column_one, column_two], axis=-1).astype(jnp.int32)


def strengthened(drawn, own_key, source, target, shards_of, factor):
    def block_of(dim):
        return (jnp.arange(drawn.shape[dim]) // (drawn.shape[dim] // shards_of)).reshape((-1,) + (1,) * (drawn.ndim - 1 - dim))

    near = jax.random.permutation(own_key, shards_of)[block_of(target)]
    other_side = (block_of(target) + shards_of // 2) % shards_of
    return jnp.where((block_of(source) == near) | (block_of(source) == other_side), factor * drawn, drawn)


def shard_levels(stream_key, shape, cuts, low, top_value):
    factor_of = 1.0
    for axis_at, blocks in cuts:
        heights = jax.random.uniform(jax.random.fold_in(jax.random.fold_in(stream_key, 6), axis_at), (blocks,), jnp.float32, low / len(cuts), top_value / len(cuts))
        factor_of = factor_of * jnp.repeat(jnp.exp(heights), shape[axis_at] // blocks).reshape((-1,) + (1,) * (len(shape) - 1 - axis_at))
    return factor_of


def noise(stream_key, dims, scale, limit, cuts=(), held_as=jnp.bfloat16):
    loudness = shard_levels(stream_key, dims, cuts, -0.22, 0.18) if cuts else 1.0
    values = jax.random.normal(stream_key, dims, jnp.float32) * scale * loudness
    return jnp.minimum(jnp.maximum(values, -limit), limit).astype(held_as)


def gaussian_with(own_key, extent, width, reach, pieces, heavy, kind=jnp.bfloat16):
    drawn = width * jax.random.normal(own_key, extent, jnp.float32)
    if pieces:
        drawn = drawn * shard_levels(own_key, extent, pieces, -0.22, 0.18)
    return jnp.clip(strengthened(drawn, jax.random.fold_in(own_key, 3), *heavy), -reach, reach).astype(kind)


def setup_inputs(seed: int = 0) -> dict:
    key_of = jax.random.split(jax.random.key(seed), 13)
    return {
        "tokens": gaussian_with(key_of[0], (MICRO, TOKENS_MB, D), 1.0, 6.0, ((1, 32),), (1, 2, 32, 2.75)),
        "cotangent": noise(key_of[1], (MICRO, TOKENS_MB, D), 1.0, 6.0, ((1, 32),)),
        "lengths": draw_lengths(jax.random.fold_in(key_of[12], 71), 0),
        "gain_attn": jnp.clip(1.0 + 0.18 * jax.random.normal(key_of[3], (D,), jnp.float32), 0.099609375, 1.8984375).astype(jnp.bfloat16),
        "w_query": noise(key_of[4], (D, HEADS * HEAD_DIM), D ** -0.5, 0.25, ((0, 8), (1, 4))),
        "w_key": noise(key_of[5], (D, KV_HEADS * HEAD_DIM), D ** -0.5, 0.25, ((0, 8), (1, 4))),
        "w_value": noise(key_of[6], (D, KV_HEADS * HEAD_DIM), D ** -0.5, 0.25, ((0, 8), (1, 4))),
        "w_out": noise(key_of[7], (HEADS * HEAD_DIM, D), (HEADS * HEAD_DIM // 64) ** -0.5, 2.0, ((0, 8), (1, 4))),
        "gain_mlp": jnp.clip(1.0 + 0.18 * jax.random.normal(key_of[8], (D,), jnp.float32), 0.099609375, 1.8984375).astype(jnp.bfloat16),
        "w_gate": noise(key_of[9], (D, FF), D ** -0.5, 0.25, ((0, 8), (1, 4))),
        "w_up": noise(key_of[10], (D, FF), D ** -0.5, 0.25, ((0, 8), (1, 4))),
        "w_down": noise(key_of[11], (FF, D), FF ** -0.5, 0.15625, ((0, 8), (1, 4))),
    }


EPSILON = 1e-05
ROPE_BASE = 100000.0
HIGHEST = lax.Precision.HIGHEST

@jax.custom_vjp
def low(v):
    return lax.optimization_barrier(v.astype(jnp.bfloat16)).astype(jnp.float32)

@jax.custom_vjp
def low_back(v):
    return v

def low_keep(v):
    return (low(v), None)

def low_pass(kept, grad):
    return (grad,)

def back_keep(v):
    return (v, None)

def back_low(kept, grad):
    return (low(grad),)
low.defvjp(low_keep, low_pass)
low_back.defvjp(back_keep, back_low)

def layout(lengths_row, token_count):
    slot_count = lengths_row.shape[0]
    ends = jnp.cumsum(lengths_row).astype(jnp.int32)
    starts = (ends - lengths_row).astype(jnp.int32)
    places = jnp.arange(token_count, dtype=jnp.int32)
    segment = lax.optimization_barrier(jnp.sum((ends[None, :] <= places[:, None]).astype(jnp.int32), axis=1)).astype(jnp.int32)
    chosen = jnp.arange(slot_count, dtype=jnp.int32)[None, :] == segment[:, None]
    begins = lax.optimization_barrier(jnp.sum(jnp.where(chosen, starts[None, :], 0), axis=1)).astype(jnp.int32)
    inside = segment < slot_count
    ident = jnp.where(inside, segment, slot_count + places).astype(jnp.int32)
    posit = jnp.where(inside, places - begins, 0).astype(jnp.int32)
    return (ident, posit)

def rope_tables(posit, halfway):
    freqs = jnp.exp(jnp.arange(halfway, dtype=jnp.float32) * (-math.log(ROPE_BASE) / halfway))
    angles = posit.astype(jnp.float32)[:, None] * freqs[None, :]
    return (jnp.cos(angles), jnp.sin(angles))

def rotate(vectors, cosine, sine):
    halfway = vectors.shape[-1] // 2
    first = vectors[..., :halfway]
    second = vectors[..., halfway:]
    cos_rows = cosine[:, None, :]
    sin_rows = sine[:, None, :]
    return jnp.concatenate([first * cos_rows - second * sin_rows, second * cos_rows + first * sin_rows], axis=-1)

def group_forward(params, inputs, lengths_row):
    gain_attn, w_query, w_key, w_value, w_out, gain_mlp, w_gate, w_up, w_down = params
    token_count = inputs.shape[0]
    ident, posit = layout(lengths_row, token_count)
    cosine, sine = rope_tables(posit, HEAD_DIM // 2)
    scale_one = lax.rsqrt(lax.optimization_barrier(jnp.mean(inputs * inputs, axis=1, keepdims=True)) + EPSILON)
    normed = low(inputs * scale_one * gain_attn)
    query_raw = low_back(jnp.dot(normed, w_query, precision=HIGHEST))
    key_raw = low_back(jnp.dot(normed, w_key, precision=HIGHEST))
    value_raw = low(low_back(jnp.dot(normed, w_value, precision=HIGHEST)))
    queries = low(rotate(query_raw.reshape(token_count, HEADS, HEAD_DIM), cosine, sine))
    keys_rot = low(rotate(key_raw.reshape(token_count, KV_HEADS, HEAD_DIM), cosine, sine))
    values_all = value_raw.reshape(token_count, KV_HEADS, HEAD_DIM)
    grouped = queries.reshape(token_count, KV_HEADS, HEADS // KV_HEADS, HEAD_DIM)
    scores = low_back(jnp.einsum('tkrd,jkd->krtj', grouped, keys_rot, precision=HIGHEST) * HEAD_DIM ** (-0.5))
    allowed = (ident[:, None] == ident[None, :]) & (posit[None, :] <= posit[:, None])
    probs = low(jax.nn.softmax(jnp.where(allowed, scores, -1e+30), axis=-1))
    attended = jnp.einsum('krtj,jkd->tkrd', probs, values_all, precision=HIGHEST).reshape(token_count, HEADS * HEAD_DIM)
    attended = low_back(low(attended))
    middle = inputs + low_back(jnp.dot(attended, w_out, precision=HIGHEST))
    scale_two = lax.rsqrt(lax.optimization_barrier(jnp.mean(middle * middle, axis=1, keepdims=True)) + EPSILON)
    normed_two = low(middle * scale_two * gain_mlp)
    gate_proj = low_back(jnp.dot(normed_two, w_gate, precision=HIGHEST))
    up_proj = low_back(jnp.dot(normed_two, w_up, precision=HIGHEST))
    hidden = low(jax.nn.silu(gate_proj) * up_proj)
    return middle + low_back(jnp.dot(hidden, w_down, precision=HIGHEST))

def reference(tokens, cotangent, lengths, gain_attn, w_query, w_key, w_value, w_out, gain_mlp, w_gate, w_up, w_down):
    params = tuple((item.astype(jnp.float32) for item in (gain_attn, w_query, w_key, w_value, w_out, gain_mlp, w_gate, w_up, w_down)))
    inputs = tokens.astype(jnp.float32).reshape(MICRO * GROUPS, GROUP_TOK, D)
    length_rows = lengths.reshape(MICRO * GROUPS, SEQS)

    def forward(weights, data):

        def one_group(pair):
            return group_forward(weights, pair[0], pair[1])
        return lax.map(jax.checkpoint(one_group), (data, length_rows))
    outputs, pull = jax.vjp(forward, params, inputs)
    grads, input_grad = pull(cotangent.astype(jnp.float32).reshape(outputs.shape))
    mixed = outputs.astype(jnp.bfloat16).reshape(tokens.shape)
    return (mixed, input_grad.reshape(tokens.shape), grads[0], grads[1], grads[2], grads[3], grads[4], grads[5], grads[6], grads[7], grads[8])
```

```python
import functools
import math

import jax
import jax.numpy as jnp
from jax import lax
from jax.experimental import pallas as pl
from jax.experimental.pallas import tpu as pltpu
from jax.sharding import PartitionSpec as P

HEADS = 9
KV_HEADS = 3
HEAD_DIM = 64
FF = 1536
REPEATS = HEADS // KV_HEADS
QW = HEADS * HEAD_DIM
KW = KV_HEADS * HEAD_DIM
EPSILON = 1e-05
ROPE_BASE = 100000.0
MASKED = -1e30
BOTH = ("dp", "fsdp")
F32 = jnp.float32
BF16 = jnp.bfloat16


def dot(a, b):
    return lax.dot_general(a, b, (((1,), (0,)), ((), ())), preferred_element_type=F32)


def dot_nt(a, b):
    return lax.dot_general(a, b, (((1,), (1,)), ((), ())), preferred_element_type=F32)


def dot_tn(a, b):
    return lax.dot_general(a, b, (((0,), (0,)), ((), ())), preferred_element_type=F32)


def params(mib=56):
    return pltpu.CompilerParams(vmem_limit_bytes=mib << 20)


def whole(count):
    return [pl.BlockSpec(memory_space=pltpu.VMEM)] * count


def pack_attention(w_query, w_key, w_value, w_out, gain_one, gain_two):
    rows = w_query.shape[0]
    body = jnp.concatenate([w.astype(F32) for w in (w_query, w_key, w_value, w_out)], axis=1)
    lanes = body.shape[1]
    extra = padded_rows(rows) - rows
    gains = jnp.concatenate(
        [
            gain_one.astype(F32),
            gain_two.astype(F32),
            jnp.zeros((1, lanes - 2 * rows), F32),
        ],
        axis=1,
    )
    gains = jnp.broadcast_to(gains, (extra, lanes))
    return jnp.concatenate([body, gains], axis=0).astype(BF16)


def padded_rows(rows):
    return -(-(rows + 1) // 16) * 16


def pack_down(w_down, rows):
    turned = w_down.astype(F32).T
    pieces = turned.shape[0] // rows
    return jnp.concatenate(
        [turned[n * rows : (n + 1) * rows] for n in range(pieces)], axis=1
    ).astype(BF16)


def unpack_attention(block, rows, q_cols, k_cols):
    block = block.astype(F32)
    ends = (0, q_cols, q_cols + k_cols, q_cols + 2 * k_cols, 2 * q_cols + 2 * k_cols)
    parts = [block[:rows, ends[n] : ends[n + 1]] for n in range(4)]
    return parts + [block[rows : rows + 1, :rows], block[rows : rows + 1, rows : 2 * rows]]


def unpack_down(block, shape):
    block = block.astype(F32)
    lanes = shape[0]
    pieces = block.shape[1] // lanes
    return jnp.concatenate(
        [block[:, n * lanes : (n + 1) * lanes] for n in range(pieces)], axis=0
    ).T


def pack_kernel(q, k, v, o, one, two, gate, up, down, attn_ref, ffn_ref):
    attn_ref[...] = pack_attention(q[...], k[...], v[...], o[...], one[...], two[...])
    ffn_ref[0] = gate[...]
    ffn_ref[1] = up[...]
    ffn_ref[2] = pack_down(down[...], gate.shape[0])


def unpack_kernel(attn, ffn, q, k, v, o, one, two, gate, up, down):
    rows = gate.shape[0]
    parts = unpack_attention(attn[...], rows, q.shape[1], k.shape[1])
    for ref, part in zip((q, k, v, o, one, two), parts, strict=True):
        ref[...] = part
    gate[...] = ffn[0].astype(F32)
    up[...] = ffn[1].astype(F32)
    down[...] = unpack_down(ffn[2], down.shape)


def attention_rows(block_of, number, members, rows, q_cols, k_cols):
    blocks = [block_of(number * members + f).astype(F32) for f in range(members)]
    ends = (0, q_cols, q_cols + k_cols, q_cols + 2 * k_cols, 2 * q_cols + 2 * k_cols)
    spans = [
        jnp.concatenate([b[:rows, ends[n] : ends[n + 1]] for b in blocks], axis=1)
        for n in range(4)
    ]
    gains = (blocks[0][rows : rows + 1, :rows], blocks[0][rows : rows + 1, rows : 2 * rows])
    return jnp.concatenate(spans[:3], axis=1), spans[3], gains


def join_attention_kernel(members, rows, q_cols, k_cols, g_ref, wqkv_ref, wo_ref, one_ref, two_ref):
    parts = g_ref.shape[0] // members
    gains = []
    for pair in range(parts // 2):
        made = [
            attention_rows(lambda n: g_ref[n], 2 * pair + s, members, rows, q_cols, k_cols)
            for s in range(2)
        ]
        gains += [m[2] for m in made]
        span = slice(pair * 2 * rows, (pair + 1) * 2 * rows)
        wqkv_ref[span, :] = jnp.concatenate([m[0] for m in made], axis=0).astype(BF16)
        wo_ref[span, :] = jnp.concatenate([m[1] for m in made], axis=0).astype(BF16)
    one_ref[...] = jnp.concatenate([g[0] for g in gains], axis=1)
    two_ref[...] = jnp.concatenate([g[1] for g in gains], axis=1)


def join_attention_plain(members, rows, q_cols, k_cols, gathered):
    parts = gathered.shape[0] // members
    made = [
        attention_rows(lambda n: gathered[n], s, members, rows, q_cols, k_cols)
        for s in range(parts)
    ]
    return (
        jnp.concatenate([m[0] for m in made], axis=0).astype(BF16),
        jnp.concatenate([m[1] for m in made], axis=0).astype(BF16),
        jnp.concatenate([m[2][0] for m in made], axis=1),
        jnp.concatenate([m[2][1] for m in made], axis=1),
    )


def join_ffn_kernel(members, g_ref, gate_ref, up_ref, down_ref):
    rows, lanes = g_ref.shape[2:]
    pairs = g_ref.shape[0] // members // 2
    half = lanes // 2
    for pair in range(pairs):
        for f in range(members):
            first = 2 * pair * members + f
            second = first + members
            for which, ref in ((0, gate_ref), (1, up_ref)):
                both = [g_ref[n, which].astype(F32) for n in (first, second)]
                ref[
                    pair * 2 * rows : (pair + 1) * 2 * rows, f * lanes : (f + 1) * lanes
                ] = jnp.concatenate(both, axis=0).astype(BF16)
            a, b = (g_ref[n, 2].astype(F32) for n in (first, second))
            top = jnp.concatenate([a[:, :half], b[:, :half]], axis=1)
            low = jnp.concatenate([a[:, half:], b[:, half:]], axis=1)
            down_ref[f * 2 * rows : (f + 1) * 2 * rows, pair * lanes : (pair + 1) * lanes] = (
                jnp.concatenate([top, low], axis=0).astype(BF16)
            )


def join_ffn_plain(members, gathered):
    rows, lanes = gathered.shape[2:]
    parts = gathered.shape[0] // members
    width = rows * parts
    g = gathered.reshape(parts, members, 3, rows, lanes)
    across = [
        g[:, :, n].transpose(0, 2, 1, 3).reshape(width, members * lanes) for n in range(2)
    ]
    deep = FF // parts
    down = g[:, :, 2].reshape(parts, members, rows, lanes // deep, deep)
    down = down.transpose(1, 3, 2, 0, 4).reshape(width, FF)
    return across[0], across[1], down


def swap_halves(chunk):
    lane = lax.broadcasted_iota(jnp.int32, chunk.shape, 1)
    low = (lane % HEAD_DIM) < HEAD_DIM // 2
    return jnp.where(low, pltpu.roll(chunk, 96, 1), pltpu.roll(chunk, 32, 1))


def turn(vectors, cosine, sine):
    chunks = []
    for n in range(vectors.shape[1] // 128):
        chunk = vectors[:, n * 128 : (n + 1) * 128]
        chunks.append(chunk * cosine + swap_halves(chunk) * sine)
    return jnp.concatenate(chunks, axis=1)


def norm_scale(values):
    return lax.rsqrt(jnp.mean(values * values, axis=1, keepdims=True) + EPSILON)


def norm_back(inputs, scale, gain, grads):
    weighted = grads * gain
    term = jnp.sum(grads * (inputs * scale), axis=0, keepdims=True)
    cubed = scale * scale * scale
    mean = jnp.mean(weighted * inputs, axis=1, keepdims=True)
    return scale * weighted - inputs * (cubed * mean), term


def pre_kernel(x_ref, w_ref, gain_ref, cos_ref, sin_ref, q_ref, kv_ref):
    x = x_ref[...].astype(F32)
    normed = (x * norm_scale(x) * gain_ref[...]).astype(BF16)
    raw = dot(normed, w_ref[...])
    turned = turn(raw[:, : QW + KW], cos_ref[...], sin_ref[...])
    q_ref[...] = (turned[:, :QW].astype(BF16).astype(F32) * HEAD_DIM**-0.5).astype(BF16)
    kv_ref[...] = jnp.concatenate([turned[:, QW:], raw[:, QW + KW :]], axis=1).astype(BF16)


def row_range(lens_ref, micro, first_row, rows):
    end_zero = lens_ref[micro, 0]
    end_one = end_zero + lens_ref[micro, 1]
    end_two = end_one + lens_ref[micro, 2]
    places = first_row + lax.broadcasted_iota(jnp.int32, (1, rows), 1)

    def begin(at):
        return jnp.where(
            at < end_zero, 0, jnp.where(at < end_one, end_zero, jnp.where(at < end_two, end_one, at))
        )

    return places, begin(places), begin(first_row)


def mask_of(key_block, rows, places, begins):
    keys = key_block * rows + lax.broadcasted_iota(jnp.int32, (rows, rows), 0)
    bias = jnp.where((keys >= begins) & (keys <= places), 0.0, MASKED)
    return jnp.concatenate([bias] * REPEATS, axis=1)


def stacked(values, group):
    first = group * REPEATS
    return jnp.concatenate(
        [
            values[:, (first + n) * HEAD_DIM : (first + n + 1) * HEAD_DIM]
            for n in range(REPEATS)
        ],
        axis=0,
    )


def unstacked(groups):
    rows = groups[0].shape[0] // REPEATS
    return jnp.concatenate(
        [g[n * rows : (n + 1) * rows] for g in groups for n in range(REPEATS)], axis=1
    )


def head_of(values, number):
    return values[:, number * HEAD_DIM : (number + 1) * HEAD_DIM]


def forward_kernel(lens_ref, place_ref, q_ref, kv_ref, out_ref, lse_ref, acc, top, total):
    micro = pl.program_id(0)
    rows = q_ref.shape[1]
    member = place_ref[0]
    places, begins, lowest = row_range(lens_ref, micro, member * rows, rows)
    queries = [stacked(q_ref[0], g) for g in range(KV_HEADS)]
    acc[...] = jnp.zeros_like(acc)
    top[...] = jnp.full_like(top, MASKED)
    total[...] = jnp.zeros_like(total)

    def block(number, carry):
        bias = mask_of(number, rows, places, begins)
        kv = kv_ref[number, 0]
        for g in range(KV_HEADS):
            keys, values = head_of(kv, g), head_of(kv, KV_HEADS + g)
            scores = dot_nt(keys, queries[g]) + bias
            before = top[g]
            now = jnp.maximum(before, jnp.max(scores, axis=0, keepdims=True))
            shrink = jnp.exp(before - now)
            weights = jnp.exp(scores - now)
            total[g] = total[g] * shrink + jnp.sum(weights, axis=0, keepdims=True)
            acc[g] = acc[g] * shrink + dot_tn(values, weights.astype(BF16))
            top[g] = now
        return carry

    lax.fori_loop(lowest // rows, member + 1, block, 0)
    done = []
    for g in range(KV_HEADS):
        done.append((acc[g] * (1.0 / total[g])).T)
        lse_ref[0, g] = top[g] + jnp.log(total[g])
    out_ref[0] = unstacked(done)


def backward_kernel(
    lens_ref, place_ref, q_ref, kv_ref, out_ref, grad_ref, lse_ref, dq_ref, dkv_ref, acc
):
    micro = pl.program_id(0)
    rows = q_ref.shape[1]
    member = place_ref[0]
    places, begins, lowest = row_range(lens_ref, micro, member * rows, rows)
    queries = [stacked(q_ref[0], g) for g in range(KV_HEADS)]
    grads = [stacked(grad_ref[0], g) for g in range(KV_HEADS)]
    product = grad_ref[0].astype(F32) * out_ref[0]
    dots = [
        jnp.sum(stacked(product, g).T, axis=0, keepdims=True) for g in range(KV_HEADS)
    ]
    acc[...] = jnp.zeros_like(acc)
    dkv_ref[...] = jnp.zeros_like(dkv_ref)

    def block(number, carry):
        bias = mask_of(number, rows, places, begins)
        kv = kv_ref[number, 0]
        grad_keys, grad_values = [], []
        for g in range(KV_HEADS):
            keys, values = head_of(kv, g), head_of(kv, KV_HEADS + g)
            probs = jnp.exp(dot_nt(keys, queries[g]) + bias - lse_ref[0, g])
            grad_probs = dot_nt(values, grads[g])
            grad_scores = (probs * (grad_probs - dots[g])).astype(BF16)
            grad_values.append(dot(probs.astype(BF16), grads[g]))
            grad_keys.append(dot(grad_scores, queries[g]))
            acc[g] = acc[g] + dot_tn(keys, grad_scores)
        dkv_ref[number, 0] = jnp.concatenate(grad_keys + grad_values, axis=1).astype(BF16)
        return carry

    lax.fori_loop(lowest // rows, member + 1, block, 0)
    dq_ref[0] = unstacked([acc[g].T for g in range(KV_HEADS)]) * HEAD_DIM**-0.5


def mid_kernel(
    members,
    as_blocks,
    x_ref,
    att_ref,
    dy_ref,
    wo_ref,
    gate_ref,
    up_ref,
    down_ref,
    gain_ref,
    mixed_ref,
    dmid_ref,
    datt_ref,
    gout_ref,
    gffn_ref,
    ggain_ref,
    s_hidden,
    s_dgate,
    s_dup,
    s_branch,
    s_normed,
    s_dy,
    s_att,
):
    step = pl.program_id(0)
    rows = x_ref.shape[0]
    here = pl.ds(pl.multiple_of(step * rows, rows), rows)
    gain = gain_ref[...]
    att = att_ref[...].astype(BF16)
    middle = x_ref[...].astype(F32) + dot(att, wo_ref[...])
    scale = norm_scale(middle)
    normed = (middle * scale * gain).astype(BF16)
    gate = dot(normed, gate_ref[...])
    up = dot(normed, up_ref[...])
    sig = lax.logistic(gate)
    silu = gate * sig
    hidden = (silu * up).astype(BF16)
    mixed_ref[...] = (middle + dot_nt(hidden, down_ref[...])).astype(BF16)
    dy = dy_ref[...]
    dhidden = dot(dy, down_ref[...])
    dgate = (dhidden * up * sig * (1.0 + gate * (1.0 - sig))).astype(BF16)
    dup = (dhidden * silu).astype(BF16)
    dnormed = dot_nt(dgate, gate_ref[...]) + dot_nt(dup, up_ref[...])
    back, term = norm_back(middle, scale, gain, dnormed)
    dmid = dy.astype(F32) + back
    dmid_ref[...] = dmid
    branch = dmid.astype(BF16)
    datt_ref[...] = dot_nt(branch, wo_ref[...]).astype(BF16)
    s_hidden[here, :] = hidden
    s_dgate[here, :] = dgate
    s_dup[here, :] = dup
    s_branch[here, :] = branch
    s_normed[here, :] = normed
    s_dy[here, :] = dy
    s_att[here, :] = att

    @pl.when(step == 0)
    def _():
        ggain_ref[...] = term

    @pl.when(step > 0)
    def _():
        ggain_ref[...] += term

    @pl.when(step == pl.num_programs(0) - 1)
    def _():
        width = s_normed.shape[1]
        gout_ref[...] = dot_tn(s_att[...], s_branch[...])
        normed_t = s_normed[...].T
        dy_t = s_dy[...].T
        if not as_blocks:
            gffn_ref[0] = dot(normed_t, s_dgate[...]).astype(BF16)
            gffn_ref[1] = dot(normed_t, s_dup[...]).astype(BF16)
            gffn_ref[2] = dot(dy_t, s_hidden[...]).astype(BF16)
            return
        parts = gffn_ref.shape[0] // members
        part = width // parts
        lanes = FF // members
        deep = FF // parts
        for f in range(members):
            for which, src in ((0, s_dgate), (1, s_dup)):
                made = dot(normed_t, src[:, f * lanes : (f + 1) * lanes])
                for n in range(parts):
                    gffn_ref[n * members + f, which] = made[n * part : (n + 1) * part].astype(BF16)
            cols = width // members
            made = dot(dy_t[f * cols : (f + 1) * cols], s_hidden[...])
            for n in range(parts):
                span = made[:, n * deep : (n + 1) * deep]
                gffn_ref[n * members + f, 2] = jnp.concatenate(
                    [span[i * part : (i + 1) * part] for i in range(cols // part)], axis=1
                ).astype(BF16)


def blocks_of_ffn(full, members, parts):
    width = full.shape[1]
    part, lanes, deep = width // parts, FF // members, FF // parts
    across = full[:2].reshape(2, parts, part, members, lanes).transpose(1, 3, 0, 2, 4)
    cols = width // members
    down = full[2].reshape(members, cols // part, part, parts, deep).transpose(3, 0, 2, 1, 4)
    across = across.reshape(parts * members, 2, part, lanes)
    down = down.reshape(parts * members, 1, part, lanes)
    return jnp.concatenate([across, down], axis=1)


def attention_blocks(grad_qkv, grad_out, gain_one, gain_two, members, parts, store):
    width = grad_qkv.shape[0]
    part = width // parts
    q_cols, k_cols = QW // members, KW // members
    extra = padded_rows(part) - part
    lanes = 2 * q_cols + 2 * k_cols
    for n in range(parts):
        rows = slice(n * part, (n + 1) * part)
        gains = jnp.concatenate(
            [gain_one[:, rows], gain_two[:, rows], jnp.zeros((1, lanes - 2 * part), F32)], axis=1
        )
        gains = jnp.broadcast_to(gains, (extra, lanes))
        for f in range(members):
            spans = [
                grad_qkv[rows, f * q_cols : (f + 1) * q_cols],
                grad_qkv[rows, QW + f * k_cols : QW + (f + 1) * k_cols],
                grad_qkv[rows, QW + KW + f * k_cols : QW + KW + (f + 1) * k_cols],
                grad_out[rows, f * q_cols : (f + 1) * q_cols],
            ]
            body = jnp.concatenate(spans, axis=1)
            store(n * members + f, jnp.concatenate([body, gains], axis=0).astype(BF16))


def post_kernel(
    members,
    as_blocks,
    x_ref,
    dq_ref,
    dkv_ref,
    dmid_ref,
    w_ref,
    gain_ref,
    cos_ref,
    sin_ref,
    gout_ref,
    ggain_ref,
    dx_ref,
    gattn_ref,
    gone_ref,
    s_raw,
    s_normed,
):
    step = pl.program_id(0)
    rows = x_ref.shape[0]
    here = pl.ds(pl.multiple_of(step * rows, rows), rows)
    gain = gain_ref[...]
    x = x_ref[...].astype(F32)
    scale = norm_scale(x)
    s_normed[here, :] = (x * scale * gain).astype(BF16)
    dkv = dkv_ref[...].astype(F32)
    turned = jnp.concatenate([dq_ref[...], dkv[:, :KW]], axis=1)
    turned = turn(turned, cos_ref[...], -sin_ref[...])
    raw = jnp.concatenate([turned, dkv[:, KW:]], axis=1).astype(BF16)
    s_raw[here, :] = raw
    back, term = norm_back(x, scale, gain, dot_nt(raw, w_ref[...]))
    dx_ref[...] = dmid_ref[...] + back

    @pl.when(step == 0)
    def _():
        gone_ref[...] = term

    @pl.when(step > 0)
    def _():
        gone_ref[...] += term

    @pl.when(step == pl.num_programs(0) - 1)
    def _():
        grad_qkv = dot_tn(s_normed[...], s_raw[...])
        if not as_blocks:
            gattn_ref[...] = grad_qkv
            return

        def store(number, block):
            gattn_ref[number] = block

        parts = gattn_ref.shape[0] // members
        attention_blocks(
            grad_qkv, gout_ref[...], gone_ref[...], ggain_ref[...], members, parts, store
        )


def shape_of(shape, dtype):
    return jax.ShapeDtypeStruct(shape, dtype)


def gather_blocks(block):
    return lax.all_gather(block, BOTH, axis=0, tiled=False)


def scatter_blocks(blocks):
    return lax.psum_scatter(blocks, BOTH, scatter_dimension=0, tiled=False)


def local(
    tokens,
    cotangent,
    lengths,
    gain_attn,
    w_query,
    w_key,
    w_value,
    w_out,
    gain_mlp,
    w_gate,
    w_up,
    w_down,
):
    members = lax.axis_size("fsdp")
    parts = lax.axis_size("dp")
    count = parts * members
    member = lax.axis_index("fsdp")
    micro, rows, width = tokens.shape
    every = micro * rows
    part = w_query.shape[0]
    q_cols, k_cols = w_query.shape[1], w_key.shape[1]
    lanes = w_gate.shape[1]
    deep = padded_rows(part)
    as_blocks = part % 8 == 0 and parts % 2 == 0 and width // members == 2 * part

    lens = lengths[:, 0, :]
    place = jnp.reshape(member, (1,)).astype(jnp.int32)
    ends = jnp.cumsum(lens, axis=1)
    at = member * rows + lax.broadcasted_iota(jnp.int32, (micro, rows), 1)
    begins = jnp.zeros_like(at)
    for n in range(lens.shape[1]):
        following = ends[:, n : n + 1] if n < lens.shape[1] - 1 else at
        begins = jnp.where(ends[:, n : n + 1] <= at, following, begins)
    posit = (at - begins).reshape(every, 1).astype(F32)
    lane = lax.broadcasted_iota(jnp.int32, (1, 128), 1)
    halfway = HEAD_DIM // 2
    freqs = jnp.exp((lane % halfway).astype(F32) * (-math.log(ROPE_BASE) / halfway))
    angles = posit * freqs
    cosine = jnp.cos(angles)
    sine = jnp.sin(angles) * jnp.where(lane % HEAD_DIM < halfway, -1.0, 1.0)

    gain_rows = (gain_attn.reshape(1, part), gain_mlp.reshape(1, part))
    own = (w_query, w_key, w_value, w_out) + gain_rows
    if as_blocks:
        attn_block, ffn_block = pl.pallas_call(
            pack_kernel,
            out_shape=(shape_of((deep, lanes), BF16), shape_of((3, part, lanes), BF16)),
            in_specs=whole(9),
            out_specs=whole(2),
            compiler_params=params(),
            name="pack",
        )(*own, w_gate, w_up, w_down)
    else:
        attn_block = pack_attention(*own)
        ffn_block = jnp.stack([w_gate, w_up, pack_down(w_down, part)])
    attn_all = gather_blocks(attn_block)
    ffn_all = gather_blocks(ffn_block)
    if as_blocks:
        wqkv, wo, gain_one, gain_two = pl.pallas_call(
            functools.partial(join_attention_kernel, members, part, q_cols, k_cols),
            out_shape=(
                shape_of((width, QW + 2 * KW), BF16),
                shape_of((QW, width), BF16),
                shape_of((1, width), F32),
                shape_of((1, width), F32),
            ),
            in_specs=whole(1),
            out_specs=whole(4),
            compiler_params=params(),
            name="join_attention",
        )(attn_all)
        gate_w, up_w, down_w = pl.pallas_call(
            functools.partial(join_ffn_kernel, members),
            out_shape=(shape_of((width, FF), BF16),) * 3,
            in_specs=whole(1),
            out_specs=whole(3),
            compiler_params=params(),
            name="join_ffn",
        )(ffn_all)
    else:
        wqkv, wo, gain_one, gain_two = join_attention_plain(
            members, part, q_cols, k_cols, attn_all
        )
        gate_w, up_w, down_w = join_ffn_plain(members, ffn_all)

    x = tokens.reshape(every, width)
    dy = cotangent.reshape(every, width)

    def by_rows(cols):
        return pl.BlockSpec((rows, cols), lambda n: (n, 0))

    def same(*shape):
        return pl.BlockSpec(shape, lambda n: (0,) * len(shape))

    queries, own_kv = pl.pallas_call(
        pre_kernel,
        grid=(micro,),
        out_shape=(shape_of((every, QW), BF16), shape_of((every, 2 * KW), BF16)),
        in_specs=[
            by_rows(width),
            same(width, QW + 2 * KW),
            same(1, width),
            by_rows(128),
            by_rows(128),
        ],
        out_specs=(by_rows(QW), by_rows(2 * KW)),
        compiler_params=params(),
        name="pre",
    )(x, wqkv, gain_one, cosine, sine)

    kv_all = lax.all_gather(own_kv, "fsdp", axis=0, tiled=False)
    kv_all = kv_all.reshape(members, micro, rows, 2 * KW)
    queries = queries.reshape(micro, rows, QW)

    smem = pl.BlockSpec(memory_space=pltpu.SMEM)
    by_micro = pl.BlockSpec((1, rows, QW), lambda n: (n, 0, 0))
    by_kv = pl.BlockSpec((members, 1, rows, 2 * KW), lambda n: (0, n, 0, 0))
    by_lse = pl.BlockSpec((1, KV_HEADS, 1, REPEATS * rows), lambda n: (n, 0, 0, 0))
    held = (KV_HEADS, HEAD_DIM, REPEATS * rows)
    line = (KV_HEADS, 1, REPEATS * rows)
    attended, logsum = pl.pallas_call(
        forward_kernel,
        grid=(micro,),
        out_shape=(shape_of((micro, rows, QW), F32), shape_of((micro,) + line, F32)),
        in_specs=[smem, smem, by_micro, by_kv],
        out_specs=(by_micro, by_lse),
        scratch_shapes=[pltpu.VMEM(held, F32), pltpu.VMEM(line, F32), pltpu.VMEM(line, F32)],
        compiler_params=params(),
        name="attend_forward",
    )(lens, place, queries, kv_all)

    if as_blocks:
        gffn_shape = (count, 3, part, lanes)
    else:
        gffn_shape = (3, width, FF)
    mixed, dmid, datt, grad_out, grad_ffn, grad_two = pl.pallas_call(
        functools.partial(mid_kernel, members, as_blocks),
        grid=(micro,),
        out_shape=(
            shape_of((every, width), BF16),
            shape_of((every, width), F32),
            shape_of((every, QW), BF16),
            shape_of((QW, width), F32),
            shape_of(gffn_shape, BF16),
            shape_of((1, width), F32),
        ),
        in_specs=[
            by_rows(width),
            by_rows(QW),
            by_rows(width),
            same(QW, width),
            same(width, FF),
            same(width, FF),
            same(width, FF),
            same(1, width),
        ],
        out_specs=(
            by_rows(width),
            by_rows(width),
            by_rows(QW),
            same(QW, width),
            same(*gffn_shape),
            same(1, width),
        ),
        scratch_shapes=[
            pltpu.VMEM((every, FF), BF16),
            pltpu.VMEM((every, FF), BF16),
            pltpu.VMEM((every, FF), BF16),
            pltpu.VMEM((every, width), BF16),
            pltpu.VMEM((every, width), BF16),
            pltpu.VMEM((every, width), BF16),
            pltpu.VMEM((every, QW), BF16),
        ],
        compiler_params=params(),
        name="mid",
    )(x, attended.reshape(every, QW), dy, wo, gate_w, up_w, down_w, gain_two)

    if not as_blocks:
        grad_ffn = blocks_of_ffn(grad_ffn, members, parts)
    ffn_sum = scatter_blocks(grad_ffn)

    dq, dkv = pl.pallas_call(
        backward_kernel,
        grid=(micro,),
        out_shape=(
            shape_of((micro, rows, QW), F32),
            shape_of((members, micro, rows, 2 * KW), BF16),
        ),
        in_specs=[smem, smem, by_micro, by_kv, by_micro, by_micro, by_lse],
        out_specs=(by_micro, by_kv),
        scratch_shapes=[pltpu.VMEM(held, F32)],
        compiler_params=params(),
        name="attend_backward",
    )(lens, place, queries, kv_all, attended, datt.reshape(micro, rows, QW), logsum)

    own_dkv = lax.psum_scatter(dkv, "fsdp", scatter_dimension=0, tiled=False)
    own_dkv = own_dkv.reshape(every, 2 * KW)

    if as_blocks:
        gattn = shape_of((count, deep, lanes), BF16)
    else:
        gattn = shape_of((width, QW + 2 * KW), F32)
    input_grad, grad_attn, grad_one = pl.pallas_call(
        functools.partial(post_kernel, members, as_blocks),
        grid=(micro,),
        out_shape=(shape_of((every, width), F32), gattn, shape_of((1, width), F32)),
        in_specs=[
            by_rows(width),
            by_rows(QW),
            by_rows(2 * KW),
            by_rows(width),
            same(width, QW + 2 * KW),
            same(1, width),
            by_rows(128),
            by_rows(128),
            same(QW, width),
            same(1, width),
        ],
        out_specs=(by_rows(width), same(*gattn.shape), same(1, width)),
        scratch_shapes=[
            pltpu.VMEM((every, QW + 2 * KW), BF16),
            pltpu.VMEM((every, width), BF16),
        ],
        compiler_params=params(),
        name="post",
    )(
        x,
        dq.reshape(every, QW),
        own_dkv,
        dmid,
        wqkv,
        gain_one,
        cosine,
        sine,
        grad_out,
        grad_two,
    )
    if not as_blocks:
        made = [None] * count

        def store(number, block):
            made[number] = block

        attention_blocks(grad_attn, grad_out, grad_one, grad_two, members, parts, store)
        grad_attn = jnp.stack(made)
    attn_sum = scatter_blocks(grad_attn)

    shapes = [
        (part, q_cols),
        (part, k_cols),
        (part, k_cols),
        w_out.shape,
        (1, part),
        (1, part),
        w_gate.shape,
        w_up.shape,
        w_down.shape,
    ]
    if as_blocks:
        grads = pl.pallas_call(
            unpack_kernel,
            out_shape=tuple(shape_of(s, F32) for s in shapes),
            in_specs=whole(2),
            out_specs=whole(9),
            compiler_params=params(),
            name="unpack",
        )(attn_sum, ffn_sum)
    else:
        grads = unpack_attention(attn_sum, part, q_cols, k_cols)
        grads += [ffn_sum[0].astype(F32), ffn_sum[1].astype(F32)]
        grads += [unpack_down(ffn_sum[2], w_down.shape)]
    return (
        mixed.reshape(tokens.shape),
        input_grad.reshape(tokens.shape),
        grads[4].reshape(-1),
        grads[0],
        grads[1],
        grads[2],
        grads[3],
        grads[5].reshape(-1),
        grads[6],
        grads[7],
        grads[8],
    )


def solution(mesh):
    rows = P(None, BOTH, None)
    block = P(*BOTH)
    gain = P("dp")
    in_specs = (rows, rows, P(None, "dp", None), gain)
    in_specs += (block, block, block, block, gain, block, block, block)
    out_specs = (rows, rows, gain, block, block, block, block, gain, block, block, block)
    return jax.shard_map(local, mesh=mesh, in_specs=in_specs, out_specs=out_specs, check_vma=False)
```

```python
import functools
import math

import jax
import jax.numpy as jnp
from jax import lax
from jax.experimental import pallas as pl
from jax.experimental.pallas import tpu as pltpu
from jax.sharding import PartitionSpec as P

HEADS = 9
KV_HEADS = 3
HEAD_DIM = 64
FF = 1536
REPEATS = HEADS // KV_HEADS
QW = HEADS * HEAD_DIM
KW = KV_HEADS * HEAD_DIM
EPSILON = 1e-05
ROPE_BASE = 100000.0
MASKED = -1e30
BOTH = ("dp", "fsdp")
F32 = jnp.float32
BF16 = jnp.bfloat16


def dot(a, b):
    return lax.dot_general(a, b, (((1,), (0,)), ((), ())), preferred_element_type=F32)


def dot_nt(a, b):
    return lax.dot_general(a, b, (((1,), (1,)), ((), ())), preferred_element_type=F32)


def dot_tn(a, b):
    return lax.dot_general(a, b, (((0,), (0,)), ((), ())), preferred_element_type=F32)


def params(mib=32):
    return pltpu.CompilerParams(vmem_limit_bytes=mib << 20)


def shape_of(shape, dtype):
    return jax.ShapeDtypeStruct(shape, dtype)


def cost(mega_flops, kilo_bytes):
    return pl.CostEstimate(
        flops=mega_flops * 1_000_000, bytes_accessed=kilo_bytes * 1000, transcendentals=0
    )


def whole(count):
    return [pl.BlockSpec(memory_space=pltpu.VMEM)] * count


def padded_rows(rows):
    return -(-(rows + 1) // 16) * 16


def padded_lanes(lanes):
    return -(-lanes // 128) * 128


def pack_attention(w_query, w_key_t, w_value_t, gain_one, gain_two):
    rows = w_query.shape[0]
    body = [w_query.astype(F32), w_key_t.astype(F32).T, w_value_t.astype(F32).T]
    used = sum(w.shape[1] for w in body)
    lanes = padded_lanes(used)
    body = jnp.concatenate(body + [jnp.zeros((rows, lanes - used), F32)], axis=1)
    gains = gain_lines(gain_one.astype(F32), gain_two.astype(F32), rows, lanes)
    return jnp.concatenate([body, gains], axis=0).astype(BF16)


def gain_lines(gain_one, gain_two, rows, lanes):
    spare = jnp.zeros((1, lanes - 2 * rows), F32)
    line = jnp.concatenate([gain_one, gain_two, spare], axis=1)
    return jnp.broadcast_to(line, (padded_rows(rows) - rows, lanes))


def pack_rest(w_gate, w_up, w_down_t, w_out):
    rows = w_gate.shape[0]
    turned = w_down_t.astype(F32)
    pieces = [turned[n * rows : (n + 1) * rows] for n in range(turned.shape[0] // rows)]
    body = [w_gate.astype(F32), w_up.astype(F32)] + pieces + [w_out.astype(F32)]
    return jnp.concatenate(body, axis=1).astype(BF16)


def unpack_attention(block, rows, q_cols, k_cols):
    ends = (0, q_cols, q_cols + k_cols, q_cols + 2 * k_cols)
    parts = [block[:rows, ends[n] : ends[n + 1]] for n in range(3)]
    gains = [block[rows : rows + 1, :rows], block[rows : rows + 1, rows : 2 * rows]]
    return [parts[0], parts[1].T, parts[2].T] + gains


def unpack_rest(block, lanes, down_shape):
    block = block.astype(F32)
    deep = down_shape[1]
    pieces = [block[:, n : n + deep] for n in range(2 * lanes, 3 * lanes, deep)]
    down = jnp.concatenate(pieces, axis=0)
    return [block[:, :lanes], block[:, lanes : 2 * lanes], down, block[:, 3 * lanes :]]


def pack_kernel(q, k, v, one, two, gate, up, down, o, attn_ref, rest_ref):
    attn_ref[...] = pack_attention(q[...], k[...], v[...], one[...], two[...])
    rest_ref[...] = pack_rest(gate[...], up[...], down[...], o[...])


def unpack_kernel(own, one_ref, two_ref, three_ref, rest, q, k, v, one, two, gate, up, down, o):
    block = own[...] + one_ref[...].astype(F32) + two_ref[...].astype(F32)
    block = block + three_ref[...].astype(F32)
    parts = unpack_attention(block, q.shape[0], q.shape[1], k.shape[0])
    parts += unpack_rest(rest[...], gate.shape[1], down.shape)
    for ref, part in zip((q, k, v, one, two, gate, up, down, o), parts, strict=True):
        ref[...] = part


def attention_rows(block_of, number, members, rows, q_cols, k_cols):
    blocks = [block_of(number * members + f).astype(F32) for f in range(members)]
    ends = (0, q_cols, q_cols + k_cols, q_cols + 2 * k_cols)
    spans = [b[:rows, ends[n] : ends[n + 1]] for n in range(3) for b in blocks]
    gains = (blocks[0][rows : rows + 1, :rows], blocks[0][rows : rows + 1, rows : 2 * rows])
    return jnp.concatenate(spans, axis=1), gains


def join_attention_kernel(members, rows, q_cols, k_cols, place_ref, *refs):
    halves, (wqkv_ref, one_ref, two_ref, blocks) = refs[:8], refs[8:]
    member, part = place_ref[0], place_ref[1]
    width = halves[0].shape[2]
    for core in range(2):
        for far in range(2):
            one, two = halves[4 * core + far], halves[4 * core + 2 + far]
            for near in range(2):
                for z in range(4):
                    other = (part ^ (2 * z + near)) * members + (member ^ (2 * far + core))
                    blocks[other, :, :width] = one[4 * near + z]
                    other = (part ^ (2 * z + far)) * members + (member ^ (2 * near + core))
                    blocks[other, :, width:] = two[4 * near + z]
    gains = []
    for pair in range(blocks.shape[0] // members // 2):
        made = [
            attention_rows(lambda n: blocks[n], 2 * pair + s, members, rows, q_cols, k_cols)
            for s in range(2)
        ]
        gains += [m[1] for m in made]
        span = slice(pair * 2 * rows, (pair + 1) * 2 * rows)
        wqkv_ref[span, :] = jnp.concatenate([m[0] for m in made], axis=0).astype(BF16)
    one_ref[...] = jnp.concatenate([g[0] for g in gains], axis=1)
    two_ref[...] = jnp.concatenate([g[1] for g in gains], axis=1)


def join_attention_plain(members, rows, q_cols, k_cols, gathered):
    parts = gathered.shape[0] // members
    made = [
        attention_rows(lambda n: gathered[n], s, members, rows, q_cols, k_cols)
        for s in range(parts)
    ]
    return (
        jnp.concatenate([m[0] for m in made], axis=0).astype(BF16),
        jnp.concatenate([m[1][0] for m in made], axis=1),
        jnp.concatenate([m[1][1] for m in made], axis=1),
    )


def join_rest_kernel(members, lanes, g_ref, gate_ref, up_ref, down_ref, wo_ref):
    rows = g_ref.shape[1]
    half = lanes // 2
    for pair in range(g_ref.shape[0] // members // 2):
        here = slice(pair * 2 * rows, (pair + 1) * 2 * rows)
        outs = []
        for f in range(members):
            first = 2 * pair * members + f
            a, b = (g_ref[n].astype(F32) for n in (first, first + members))
            cols = slice(f * lanes, (f + 1) * lanes)
            gate_ref[here, cols] = jnp.concatenate([a[:, :lanes], b[:, :lanes]], axis=0).astype(
                BF16
            )
            up_ref[here, cols] = jnp.concatenate(
                [a[:, lanes : 2 * lanes], b[:, lanes : 2 * lanes]], axis=0
            ).astype(BF16)
            outs.append(jnp.concatenate([a[:, 3 * lanes :], b[:, 3 * lanes :]], axis=0))
            a, b = a[:, 2 * lanes : 3 * lanes], b[:, 2 * lanes : 3 * lanes]
            top = jnp.concatenate([a[:, :half], b[:, :half]], axis=1)
            low = jnp.concatenate([a[:, half:], b[:, half:]], axis=1)
            down_ref[f * 2 * rows : (f + 1) * 2 * rows, pair * lanes : (pair + 1) * lanes] = (
                jnp.concatenate([top, low], axis=0).astype(BF16)
            )
        wo_ref[here, :] = jnp.concatenate(outs, axis=1).astype(BF16)


def join_rest_plain(members, lanes, gathered):
    rows = gathered.shape[1]
    parts = gathered.shape[0] // members
    width = rows * parts
    g = gathered.reshape(parts, members, rows, gathered.shape[2])
    deep = FF // parts

    def across(first, last):
        piece = g[..., first:last].transpose(0, 2, 1, 3)
        return piece.reshape(width, members * (last - first))

    down = g[..., 2 * lanes : 3 * lanes].reshape(parts, members, rows, lanes // deep, deep)
    down = down.transpose(1, 3, 2, 0, 4).reshape(width, FF)
    return across(0, lanes), across(lanes, 2 * lanes), down, across(3 * lanes, g.shape[3])


def swap(value, axis, bit):
    size = lax.axis_size(axis)
    return lax.ppermute(value, axis, [(n, n ^ bit) for n in range(size)])


def bundle_one_kernel(own, one, two, three, a_ref, b_ref):
    half = own.shape[1] // 2
    for n, ref in enumerate((own, one, two, three)):
        a_ref[n] = ref[:, :half]
        b_ref[n] = ref[:, half:]


def bundle_two_kernel(a, a_far, b, b_far, a_ref, b_ref):
    for out, parts in ((a_ref, (a, a_far)), (b_ref, (b, b_far))):
        for n, ref in enumerate(parts):
            out[n * 4 : (n + 1) * 4] = ref[...]


def gather_attention(block, early):
    rows, lanes = block.shape
    half = lanes // 2

    def bundled(kernel, count, *values):
        return pl.pallas_call(
            kernel,
            out_shape=(shape_of((count, rows, half), BF16),) * 2,
            in_specs=whole(4),
            out_specs=whole(2),
            compiler_params=params(),
            cost_estimate=cost(1, 1500),
            name="bundle",
        )(*values)

    along = [swap(block, "dp", 2 * n) for n in (1, 2, 3)]
    along, early = lax.optimization_barrier((along, early))
    a, b = bundled(bundle_one_kernel, 4, block, *along)
    a, b = bundled(bundle_two_kernel, 8, a, swap(a, "dp", 1), b, swap(b, "fsdp", 2))
    a_far, b_far = swap(a, "fsdp", 2), swap(b, "dp", 1)
    mine = (a, a_far, b, b_far)
    return mine + tuple(swap(value, "fsdp", 1) for value in mine), early


def add(a, b):
    return a.astype(F32) + b.astype(F32)


def reduce_one_kernel(a, a_got, b, b_got, a_keep, a_send, b_keep, b_send):
    for own, got, keep, send in ((a, a_got, a_keep, a_send), (b, b_got, b_keep, b_send)):
        keep[...] = add(own[0], got[0]).astype(BF16)
        send[...] = add(own[1], got[1]).astype(BF16)


def reduce_two_kernel(a, a_got, b, b_got, a_keep, a_send, b_keep, b_send):
    for own, got, keep, send in ((a, a_got, a_keep, a_send), (b, b_got, b_keep, b_send)):
        keep[...] = add(own[:4], got[:4]).astype(BF16)
        send[...] = add(own[4:], got[4:]).astype(BF16)


def reduce_three_kernel(a, a_got, b, b_got, own_ref, one, two, three):
    for n, ref in enumerate((own_ref, one, two, three)):
        made = jnp.concatenate([add(a[n], a_got[n]), add(b[n], b_got[n])], axis=1)
        ref[...] = made.astype(ref.dtype)


def reduce_attention(a_keep, a_send, b_keep, b_send):
    rows, half = a_keep.shape[2:]

    def call(kernel, shapes, *values):
        return pl.pallas_call(
            kernel,
            out_shape=shapes,
            in_specs=whole(4),
            out_specs=whole(4),
            compiler_params=params(),
            cost_estimate=cost(1, 3000),
            name="reduce",
        )(*values)

    a_got, b_got = swap(a_send, "fsdp", 1), swap(b_send, "fsdp", 1)
    shapes = (shape_of((8, rows, half), BF16),) * 4
    a_keep, a_send, b_keep, b_send = call(
        reduce_one_kernel, shapes, a_keep, a_got, b_keep, b_got
    )
    a_got, b_got = swap(a_send, "fsdp", 2), swap(b_send, "dp", 1)
    shapes = (shape_of((4, rows, half), BF16),) * 4
    a_keep, a_send, b_keep, b_send = call(
        reduce_two_kernel, shapes, a_keep, a_got, b_keep, b_got
    )
    a_got, b_got = swap(a_send, "dp", 1), swap(b_send, "fsdp", 2)
    shapes = (shape_of((rows, 2 * half), F32),) + (shape_of((rows, 2 * half), BF16),) * 3
    own, *send = call(reduce_three_kernel, shapes, a_keep, a_got, b_keep, b_got)
    return [own] + [swap(value, "dp", 2 * n) for n, value in zip((1, 2, 3), send)]


def swap_halves(chunk):
    lane = lax.broadcasted_iota(jnp.int32, chunk.shape, 1)
    low = (lane % HEAD_DIM) < HEAD_DIM // 2
    return jnp.where(low, pltpu.roll(chunk, 96, 1), pltpu.roll(chunk, 32, 1))


def turn(vectors, cosine, sine):
    chunks = []
    for n in range(vectors.shape[1] // 128):
        chunk = vectors[:, n * 128 : (n + 1) * 128]
        chunks.append(chunk * cosine + swap_halves(chunk) * sine)
    return jnp.concatenate(chunks, axis=1)


def norm_scale(values):
    return lax.rsqrt(jnp.mean(values * values, axis=1, keepdims=True) + EPSILON)


def norm_back(inputs, scale, gain, grads):
    weighted = grads * gain
    term = jnp.sum(grads * (inputs * scale), axis=0, keepdims=True)
    cubed = scale * scale * scale
    mean = jnp.mean(weighted * inputs, axis=1, keepdims=True)
    return scale * weighted - inputs * (cubed * mean), term


def pre_kernel(x_ref, w_ref, gain_ref, cos_ref, sin_ref, q_ref, kv_ref):
    x = x_ref[...].astype(F32)
    normed = (x * norm_scale(x) * gain_ref[...]).astype(BF16)
    raw = dot(normed, w_ref[...])
    turned = turn(raw[:, : QW + KW], cos_ref[...], sin_ref[...])
    q_ref[...] = (turned[:, :QW].astype(BF16).astype(F32) * HEAD_DIM**-0.5).astype(BF16)
    kv_ref[...] = jnp.concatenate([turned[:, QW:], raw[:, QW + KW :]], axis=1).astype(BF16)


def row_range(lens_ref, micro, first_row, rows):
    end_zero = lens_ref[micro, 0]
    end_one = end_zero + lens_ref[micro, 1]
    end_two = end_one + lens_ref[micro, 2]
    places = first_row + lax.broadcasted_iota(jnp.int32, (1, rows), 1)

    def begin(at):
        return jnp.where(
            at < end_zero, 0, jnp.where(at < end_one, end_zero, jnp.where(at < end_two, end_one, at))
        )

    return places, begin(places), begin(first_row)


def mask_of(key_block, rows, places, begins):
    keys = key_block * rows + lax.broadcasted_iota(jnp.int32, (rows, rows), 0)
    bias = jnp.where((keys >= begins) & (keys <= places), 0.0, MASKED)
    return jnp.concatenate([bias] * REPEATS, axis=1)


def stacked(values, group):
    first = group * REPEATS
    return jnp.concatenate(
        [
            values[:, (first + n) * HEAD_DIM : (first + n + 1) * HEAD_DIM]
            for n in range(REPEATS)
        ],
        axis=0,
    )


def unstacked(groups):
    rows = groups[0].shape[0] // REPEATS
    return jnp.concatenate(
        [g[n * rows : (n + 1) * rows] for g in groups for n in range(REPEATS)], axis=1
    )


def head_of(values, number):
    return values[:, number * HEAD_DIM : (number + 1) * HEAD_DIM]


def place_kv(member, refs, kv):
    for distance, ref in enumerate(refs):
        kv[member ^ distance] = ref[...]


def forward_kernel(
    micro, lens_ref, place_ref, q_ref, kv_0, kv_1, kv_2, kv_3, out_ref, lse_ref, kv, acc, top, total
):
    rows = q_ref.shape[0]
    member = place_ref[0]
    places, begins, lowest = row_range(lens_ref, micro, member * rows, rows)
    place_kv(member, (kv_0, kv_1, kv_2, kv_3), kv)
    queries = [stacked(q_ref[...], g) for g in range(KV_HEADS)]
    acc[...] = jnp.zeros_like(acc)
    top[...] = jnp.full_like(top, MASKED)
    total[...] = jnp.zeros_like(total)

    def block(number, carry):
        bias = mask_of(number, rows, places, begins)
        both = kv[number]
        for g in range(KV_HEADS):
            keys, values = head_of(both, g), head_of(both, KV_HEADS + g)
            scores = dot_nt(keys, queries[g]) + bias
            before = top[g]
            now = jnp.maximum(before, jnp.max(scores, axis=0, keepdims=True))
            shrink = jnp.exp(before - now)
            weights = jnp.exp(scores - now)
            total[g] = total[g] * shrink + jnp.sum(weights, axis=0, keepdims=True)
            acc[g] = acc[g] * shrink + dot_tn(values, weights.astype(BF16))
            top[g] = now
        return carry

    lax.fori_loop(lowest // rows, member + 1, block, 0)
    done = []
    for g in range(KV_HEADS):
        done.append((acc[g] * (1.0 / total[g])).T)
        lse_ref[g] = top[g] + jnp.log(total[g])
    out_ref[...] = unstacked(done)


def backward_kernel(
    micro,
    lens_ref,
    place_ref,
    q_ref,
    kv_0,
    kv_1,
    kv_2,
    kv_3,
    out_ref,
    grad_ref,
    lse_ref,
    dq_ref,
    own_ref,
    far_ref,
    send_ref,
    kv,
    dkv,
    acc,
):
    rows = q_ref.shape[0]
    member = place_ref[0]
    places, begins, lowest = row_range(lens_ref, micro, member * rows, rows)
    place_kv(member, (kv_0, kv_1, kv_2, kv_3), kv)
    queries = [stacked(q_ref[...], g) for g in range(KV_HEADS)]
    grads = [stacked(grad_ref[...], g) for g in range(KV_HEADS)]
    product = grad_ref[...].astype(F32) * out_ref[...]
    dots = [jnp.sum(stacked(product, g).T, axis=0, keepdims=True) for g in range(KV_HEADS)]
    acc[...] = jnp.zeros_like(acc)
    dkv[...] = jnp.zeros_like(dkv)

    def block(number, carry):
        bias = mask_of(number, rows, places, begins)
        both = kv[number]
        grad_keys, grad_values = [], []
        for g in range(KV_HEADS):
            keys, values = head_of(both, g), head_of(both, KV_HEADS + g)
            probs = jnp.exp(dot_nt(keys, queries[g]) + bias - lse_ref[g])
            grad_probs = dot_nt(values, grads[g])
            grad_scores = (probs * (grad_probs - dots[g])).astype(BF16)
            grad_values.append(dot(probs.astype(BF16), grads[g]))
            grad_keys.append(dot(grad_scores, queries[g]))
            acc[g] = acc[g] + dot_tn(keys, grad_scores)
        dkv[number ^ member] = jnp.concatenate(grad_keys + grad_values, axis=1).astype(BF16)
        return carry

    lax.fori_loop(lowest // rows, member + 1, block, 0)
    dq_ref[...] = unstacked([acc[g].T for g in range(KV_HEADS)]) * HEAD_DIM**-0.5
    own_ref[...] = dkv[0]
    far_ref[...] = dkv[2]
    send_ref[0] = dkv[1]
    send_ref[1] = dkv[3]


def mid_kernel(
    members,
    as_blocks,
    x_ref,
    att_0,
    att_1,
    att_2,
    dy_ref,
    wo_ref,
    gate_ref,
    up_ref,
    down_ref,
    gain_ref,
    mixed_ref,
    dmid_ref,
    datt_ref,
    gffn_ref,
    ggain_ref,
    s_hidden,
    s_dgate,
    s_dup,
    s_branch,
    s_normed,
    s_dy,
    s_att,
):
    step = pl.program_id(0)
    rows = x_ref.shape[0]
    here = pl.ds(pl.multiple_of(step * rows, rows), rows)
    gain = gain_ref[...]
    for n, ref in enumerate((att_0, att_1, att_2)):

        @pl.when(step == n)
        def _(ref=ref):
            s_att[here, :] = ref[...].astype(BF16)

    att = s_att[here, :]
    middle = x_ref[...].astype(F32) + dot(att, wo_ref[...])
    scale = norm_scale(middle)
    normed = (middle * scale * gain).astype(BF16)
    dy = dy_ref[...]
    out, dnormed = middle, 0.0
    for first in range(0, FF, FF // 2):
        cols = slice(first, first + FF // 2)
        gate = dot(normed, gate_ref[:, cols])
        up = dot(normed, up_ref[:, cols])
        sig = lax.logistic(gate)
        silu = gate * sig
        hidden = (silu * up).astype(BF16)
        s_hidden[here, cols] = hidden
        out = out + dot_nt(hidden, down_ref[:, cols])
        dhidden = dot(dy, down_ref[:, cols])
        dgate = (dhidden * up * sig * (1.0 + gate * (1.0 - sig))).astype(BF16)
        dup = (dhidden * silu).astype(BF16)
        s_dgate[here, cols] = dgate
        s_dup[here, cols] = dup
        dnormed = dnormed + dot_nt(dgate, gate_ref[:, cols]) + dot_nt(dup, up_ref[:, cols])
    mixed_ref[0] = out.T.astype(BF16)
    back, term = norm_back(middle, scale, gain, dnormed)
    dmid = dy.astype(F32) + back
    dmid_ref[...] = dmid
    branch = dmid.astype(BF16)
    datt_ref[...] = dot_nt(branch, wo_ref[...]).astype(BF16)
    s_branch[here, :] = branch
    s_normed[here, :] = normed
    s_dy[here, :] = dy

    @pl.when(step == 0)
    def _():
        ggain_ref[...] = term

    @pl.when(step > 0)
    def _():
        ggain_ref[...] += term

    @pl.when(step == pl.num_programs(0) - 1)
    def _():
        width = s_normed.shape[1]
        grad_out = dot_tn(s_att[...], s_branch[...])
        normed_t = s_normed[...].T
        dy_t = s_dy[...].T
        if not as_blocks:
            gffn_ref[:, :FF] = dot(normed_t, s_dgate[...]).astype(BF16)
            gffn_ref[:, FF : 2 * FF] = dot(normed_t, s_dup[...]).astype(BF16)
            gffn_ref[:, 2 * FF : 3 * FF] = dot(dy_t, s_hidden[...]).astype(BF16)
            gffn_ref[:, 3 * FF :] = grad_out.astype(BF16)
            return
        parts = gffn_ref.shape[0] // members
        part = width // parts
        lanes = FF // members
        deep = FF // parts
        cols = width // members
        for f in range(members):
            for which, src in ((0, s_dgate), (1, s_dup)):
                made = dot(normed_t, src[:, f * lanes : (f + 1) * lanes])
                for n in range(parts):
                    gffn_ref[n * members + f, :, which * lanes : (which + 1) * lanes] = made[
                        n * part : (n + 1) * part
                    ].astype(BF16)
            made = dot(dy_t[f * cols : (f + 1) * cols], s_hidden[...])
            for n in range(parts):
                span = made[:, n * deep : (n + 1) * deep]
                gffn_ref[n * members + f, :, 2 * lanes : 3 * lanes] = jnp.concatenate(
                    [span[i * part : (i + 1) * part] for i in range(cols // part)], axis=1
                ).astype(BF16)
                gffn_ref[n * members + f, :, 3 * lanes :] = grad_out[
                    n * part : (n + 1) * part, f * cols : (f + 1) * cols
                ].astype(BF16)


def blocks_of_rest(full, members, parts):
    width = full.shape[0]
    part, lanes, deep = width // parts, FF // members, FF // parts
    cols = width // members

    def across(first, last):
        piece = full[:, first:last].reshape(parts, part, members, (last - first) // members)
        return piece.transpose(0, 2, 1, 3)

    down = full[:, 2 * FF : 3 * FF].reshape(members, cols // part, part, parts, deep)
    down = down.transpose(3, 0, 2, 1, 4).reshape(parts, members, part, lanes)
    made = [across(0, FF), across(FF, 2 * FF), down, across(3 * FF, full.shape[1])]
    made = jnp.concatenate(made, axis=3)
    return made.reshape(parts * members, part, made.shape[3])


def post_kernel(
    x_ref,
    dq_ref,
    own_ref,
    near_ref,
    far_ref,
    dmid_ref,
    w_ref,
    gain_ref,
    cos_ref,
    sin_ref,
    held_ref,
    dx_ref,
    raw_ref,
    normed_ref,
    term_ref,
):
    gain = gain_ref[...]
    x = x_ref[...].astype(F32)
    scale = norm_scale(x)
    normed_ref[...] = (x * scale * gain).astype(BF16)
    dkv = add(own_ref[...], near_ref[0]) + far_ref[...].astype(F32)
    turned = jnp.concatenate([dq_ref[...], dkv[:, :KW]], axis=1)
    turned = turn(turned, cos_ref[...], -sin_ref[...])
    raw = jnp.concatenate([turned, dkv[:, KW:]], axis=1).astype(BF16)
    raw_ref[...] = raw
    back, term = norm_back(x, scale, gain, dot_nt(raw, w_ref[...]))
    dx_ref[0] = (dmid_ref[...] + back).T
    term_ref[...] = term


def attention_blocks(grad_qkv, gain_one, gain_two, members, parts, store):
    width = grad_qkv.shape[0]
    part = width // parts
    q_cols, k_cols = QW // members, KW // members
    used = q_cols + 2 * k_cols
    lanes = padded_lanes(used)
    spare = jnp.zeros((part, lanes - used), F32)
    for n in range(parts):
        rows = slice(n * part, (n + 1) * part)
        gains = gain_lines(gain_one[:, rows], gain_two[:, rows], part, lanes)
        for f in range(members):
            spans = [
                grad_qkv[rows, f * q_cols : (f + 1) * q_cols],
                grad_qkv[rows, QW + f * k_cols : QW + (f + 1) * k_cols],
                grad_qkv[rows, QW + KW + f * k_cols : QW + KW + (f + 1) * k_cols],
                spare,
            ]
            body = jnp.concatenate(spans, axis=1)
            store(n, f, jnp.concatenate([body, gains], axis=0).astype(BF16))


def grads_kernel(members, parts, *refs):
    place_ref, raws, normeds, terms = refs[0], refs[1:4], refs[4:7], refs[7:10]
    gain_two_ref, outs = refs[10], refs[11:]
    raw = jnp.concatenate([r[...] for r in raws], axis=0)
    normed = jnp.concatenate([r[...] for r in normeds], axis=0)
    grad_qkv = dot_tn(normed, raw)
    gain_one = terms[0][...] + terms[1][...] + terms[2][...]
    if len(outs) == 2:
        outs[0][...] = grad_qkv
        outs[1][...] = gain_one
        return
    a_keep, a_send, b_keep, b_send, s_a, s_b = outs
    member, place = place_ref[0], place_ref[1]
    half = s_a.shape[4]

    def store(n, f, block):
        away = place ^ n
        x, z = away & 1, away >> 1
        away = member ^ f
        core, y = away & 1, away >> 1
        s_a[core, y, 4 * x + z] = block[:, :half]
        s_b[core, x, 4 * y + z] = block[:, half:]

    attention_blocks(grad_qkv, gain_one, gain_two_ref[...], members, parts, store)
    a_keep[...] = s_a[0]
    a_send[...] = s_a[1]
    b_keep[...] = s_b[0]
    b_send[...] = s_b[1]


def local(
    tokens,
    cotangent,
    lengths,
    gain_attn,
    w_query,
    w_key,
    w_value,
    w_out,
    gain_mlp,
    w_gate,
    w_up,
    w_down,
):
    members = lax.axis_size("fsdp")
    parts = lax.axis_size("dp")
    count = parts * members
    member = lax.axis_index("fsdp")
    micro, rows, width = tokens.shape
    every = micro * rows
    part = w_query.shape[0]
    q_cols, k_cols = w_query.shape[1], w_key.shape[1]
    lanes = w_gate.shape[1]
    deep = padded_rows(part)
    attn_lanes = padded_lanes(q_cols + 2 * k_cols)
    rest_lanes = 3 * lanes + w_out.shape[1]
    as_blocks = parts == 8 and part % 8 == 0 and width // members == 2 * part

    lens = lengths[:, 0, :]
    place = jnp.stack([member, lax.axis_index("dp")]).astype(jnp.int32)
    ends = jnp.cumsum(lens, axis=1)
    at = member * rows + lax.broadcasted_iota(jnp.int32, (micro, rows), 1)
    begins = jnp.zeros_like(at)
    for n in range(lens.shape[1]):
        following = ends[:, n : n + 1] if n < lens.shape[1] - 1 else at
        begins = jnp.where(ends[:, n : n + 1] <= at, following, begins)
    posit = (at - begins).reshape(every, 1).astype(F32)
    lane = lax.broadcasted_iota(jnp.int32, (1, 128), 1)
    halfway = HEAD_DIM // 2
    freqs = jnp.exp((lane % halfway).astype(F32) * (-math.log(ROPE_BASE) / halfway))
    angles = posit * freqs
    cosine = jnp.cos(angles)
    sine = jnp.sin(angles) * jnp.where(lane % HEAD_DIM < halfway, -1.0, 1.0)

    gain_rows = (gain_attn.reshape(1, part), gain_mlp.reshape(1, part))
    own = (w_query, w_key.T, w_value.T) + gain_rows
    others = (w_gate, w_up, w_down.T, w_out)
    if as_blocks:
        attn_block, rest_block = pl.pallas_call(
            pack_kernel,
            out_shape=(
                shape_of((deep, attn_lanes), BF16),
                shape_of((part, rest_lanes), BF16),
            ),
            in_specs=whole(9),
            out_specs=whole(2),
            compiler_params=params(),
            cost_estimate=cost(1, 500),
            name="pack",
        )(*own, *others)
    else:
        attn_block, rest_block = pack_attention(*own), pack_rest(*others)
    rest_all = lax.all_gather(rest_block, BOTH, axis=0, tiled=False)
    smem = pl.BlockSpec(memory_space=pltpu.SMEM)
    x = tokens.reshape(every, width)
    dy = cotangent.reshape(every, width)
    if as_blocks:
        gathered, early = gather_attention(attn_block, (cosine, sine, x))
        cosine, sine, x = early
        wqkv, gain_one, gain_two = pl.pallas_call(
            functools.partial(join_attention_kernel, members, part, q_cols, k_cols),
            out_shape=(
                shape_of((width, QW + 2 * KW), BF16),
                shape_of((1, width), F32),
                shape_of((1, width), F32),
            ),
            in_specs=[smem] + whole(8),
            out_specs=whole(3),
            scratch_shapes=[pltpu.VMEM((count, deep, attn_lanes), BF16)],
            compiler_params=params(),
            cost_estimate=cost(10, 6000),
            name="join_attention",
        )(place, *gathered)
        gate_w, up_w, down_w, wo = pl.pallas_call(
            functools.partial(join_rest_kernel, members, lanes),
            out_shape=(shape_of((width, FF), BF16),) * 3 + (shape_of((QW, width), BF16),),
            in_specs=whole(1),
            out_specs=whole(4),
            compiler_params=params(),
            cost_estimate=cost(10, 14000),
            name="join_rest",
        )(rest_all)
    else:
        attn_all = lax.all_gather(attn_block, BOTH, axis=0, tiled=False)
        wqkv, gain_one, gain_two = join_attention_plain(members, part, q_cols, k_cols, attn_all)
        gate_w, up_w, down_w, wo = join_rest_plain(members, lanes, rest_all)

    def by_rows(cols):
        return pl.BlockSpec((rows, cols), lambda n: (n, 0))

    def same(*shape):
        return pl.BlockSpec(shape, lambda n: (0,) * len(shape))

    def once(*shape):
        return pl.BlockSpec(
            shape, lambda n: (0,) * len(shape), pipeline_mode=pl.Buffered(buffer_count=1)
        )

    def only(number, cols):
        return pl.BlockSpec((rows, cols), lambda n: (number, 0))

    def turned(number):
        return pl.BlockSpec((1, width, rows), lambda n: (number, 0, 0))

    held = pltpu.VMEM((KV_HEADS, HEAD_DIM, REPEATS * rows), F32)
    line = (KV_HEADS, 1, REPEATS * rows)
    kv_blocks = pltpu.VMEM((members, rows, 2 * KW), BF16)
    kv_block = same(rows, 2 * KW)
    outward = [(0, 2), (1, 3)]
    queries, kvs = [], []
    for m in range(micro):
        query, kv = pl.pallas_call(
            pre_kernel,
            grid=(1,),
            out_shape=(shape_of((rows, QW), BF16), shape_of((rows, 2 * KW), BF16)),
            in_specs=[
                only(m, width),
                same(width, QW + 2 * KW),
                same(1, width),
                only(m, 128),
                only(m, 128),
            ],
            out_specs=(same(rows, QW), same(rows, 2 * KW)),
            compiler_params=params(),
            cost_estimate=cost(500, 6000),
            name="pre",
        )(x, wqkv, gain_one, cosine, sine)
        far = lax.ppermute(kv, "fsdp", outward)
        queries.append(query)
        kvs.append((kv, swap(kv, "fsdp", 1), far, swap(far, "fsdp", 1)))

    attended, logsums = [], []
    for m in range(micro):
        out, logsum = pl.pallas_call(
            functools.partial(forward_kernel, m),
            grid=(1,),
            out_shape=(shape_of((rows, QW), F32), shape_of(line, F32)),
            in_specs=[smem, smem, same(rows, QW)] + [kv_block] * 4,
            out_specs=(same(rows, QW), same(*line)),
            scratch_shapes=[kv_blocks, held, pltpu.VMEM(line, F32), pltpu.VMEM(line, F32)],
            compiler_params=params(),
            cost_estimate=cost(8000, 4000),
            name="attend_forward",
        )(lens, place, queries[m], *kvs[m])
        attended.append(out)
        logsums.append(logsum)

    grad_shape = (count, part, rest_lanes) if as_blocks else (width, 3 * FF + width)
    mixed, dmid, datt, grad_rest, grad_two = pl.pallas_call(
        functools.partial(mid_kernel, members, as_blocks),
        grid=(micro,),
        out_shape=(
            shape_of((micro, width, rows), BF16),
            shape_of((every, width), F32),
            shape_of((every, QW), BF16),
            shape_of(grad_shape, BF16),
            shape_of((1, width), F32),
        ),
        in_specs=[by_rows(width)]
        + [once(rows, QW)] * 3
        + [
            by_rows(width),
            once(QW, width),
            once(width, FF),
            once(width, FF),
            once(width, FF),
            once(1, width),
        ],
        out_specs=(
            pl.BlockSpec((1, width, rows), lambda n: (n, 0, 0)),
            by_rows(width),
            by_rows(QW),
            same(*grad_shape),
            same(1, width),
        ),
        scratch_shapes=[
            pltpu.VMEM((every, FF), BF16),
            pltpu.VMEM((every, FF), BF16),
            pltpu.VMEM((every, FF), BF16),
            pltpu.VMEM((every, width), BF16),
            pltpu.VMEM((every, width), BF16),
            pltpu.VMEM((every, width), BF16),
            pltpu.VMEM((every, QW), BF16),
        ],
        compiler_params=params(48),
        cost_estimate=cost(40000, 40000),
        name="mid",
    )(x, *attended, dy, wo, gate_w, up_w, down_w, gain_two)

    if not as_blocks:
        grad_rest = blocks_of_rest(grad_rest, members, parts)
    rest_sum = lax.psum_scatter(grad_rest, BOTH, scatter_dimension=0, tiled=False)

    back = []
    for m in range(micro):
        dq, keep, far, send = pl.pallas_call(
            functools.partial(backward_kernel, m),
            grid=(1,),
            out_shape=(
                shape_of((rows, QW), F32),
                shape_of((rows, 2 * KW), BF16),
                shape_of((rows, 2 * KW), BF16),
                shape_of((2, rows, 2 * KW), BF16),
            ),
            in_specs=[smem, smem, same(rows, QW)]
            + [kv_block] * 4
            + [same(rows, QW), only(m, QW), same(*line)],
            out_specs=(same(rows, QW), kv_block, kv_block, same(2, rows, 2 * KW)),
            scratch_shapes=[kv_blocks, kv_blocks, held],
            compiler_params=params(),
            cost_estimate=cost(11000, 5000),
            name="attend_backward",
        )(lens, place, queries[m], *kvs[m], attended[m], datt, logsums[m])
        near = swap(send, "fsdp", 1)
        far = add(far, near[1]).astype(BF16)
        far = lax.ppermute(far, "fsdp", [(b, a) for a, b in outward])
        back.append((dq, keep, near, far))

    input_grad = jnp.zeros((micro, width, rows), F32)
    raws, normeds, terms = [], [], []
    for m in range(micro):
        dq, keep, near, far = back[m]
        input_grad, raw, normed, term = pl.pallas_call(
            post_kernel,
            grid=(1,),
            out_shape=(
                shape_of((micro, width, rows), F32),
                shape_of((rows, QW + 2 * KW), BF16),
                shape_of((rows, width), BF16),
                shape_of((1, width), F32),
            ),
            in_specs=[
                only(m, width),
                same(rows, QW),
                kv_block,
                pl.BlockSpec((1, rows, 2 * KW), lambda n: (0, 0, 0)),
                kv_block,
                only(m, width),
                same(width, QW + 2 * KW),
                same(1, width),
                only(m, 128),
                only(m, 128),
                pl.BlockSpec(memory_space=pl.ANY),
            ],
            out_specs=(
                turned(m),
                same(rows, QW + 2 * KW),
                same(rows, width),
                same(1, width),
            ),
            input_output_aliases={10: 0},
            compiler_params=params(),
            cost_estimate=cost(2000, 8000),
            name="post",
        )(x, dq, keep, near, far, dmid, wqkv, gain_one, cosine, sine, input_grad)
        raws.append(raw)
        normeds.append(normed)
        terms.append(term)

    if as_blocks:
        made = (shape_of((2, 8, deep, attn_lanes // 2), BF16),) * 4
        scratch = [pltpu.VMEM((2, 2, 8, deep, attn_lanes // 2), BF16)] * 2
    else:
        made = (shape_of((width, QW + 2 * KW), F32), shape_of((1, width), F32))
        scratch = []
    made = pl.pallas_call(
        functools.partial(grads_kernel, members, parts),
        out_shape=made,
        in_specs=[smem] + whole(10),
        out_specs=whole(len(made)),
        scratch_shapes=scratch,
        compiler_params=params(),
        cost_estimate=cost(3000, 8000),
        name="grads",
    )(place, *raws, *normeds, *terms, grad_two)

    if as_blocks:
        shapes = [
            (part, q_cols),
            (k_cols, part),
            (k_cols, part),
            (1, part),
            (1, part),
            w_gate.shape,
            w_up.shape,
            w_down.shape[::-1],
            w_out.shape,
        ]
        grads = pl.pallas_call(
            unpack_kernel,
            out_shape=tuple(shape_of(s, F32) for s in shapes),
            in_specs=whole(5),
            out_specs=whole(9),
            compiler_params=params(),
            cost_estimate=cost(1, 3000),
            name="unpack",
        )(*reduce_attention(*made), rest_sum)
    else:
        blocks = []
        attention_blocks(
            made[0], made[1], grad_two, members, parts, lambda n, f, block: blocks.append(block)
        )
        attn_sum = lax.psum_scatter(
            jnp.stack(blocks), BOTH, scatter_dimension=0, tiled=False
        ).astype(F32)
        grads = unpack_attention(attn_sum, part, q_cols, k_cols)
        grads += unpack_rest(rest_sum, lanes, w_down.shape[::-1])
    g_query, g_key, g_value, g_one, g_two, g_gate, g_up, g_down, g_out = grads
    return (
        mixed.transpose(0, 2, 1),
        input_grad.transpose(0, 2, 1),
        g_one.reshape(-1),
        g_query,
        g_key.T,
        g_value.T,
        g_out,
        g_two.reshape(-1),
        g_gate,
        g_up,
        g_down.T,
    )


def solution(mesh):
    rows = P(None, BOTH, None)
    block = P(*BOTH)
    gain = P("dp")
    in_specs = (rows, rows, P(None, "dp", None), gain)
    in_specs += (block, block, block, block, gain, block, block, block)
    out_specs = (rows, rows, gain, block, block, block, block, gain, block, block, block)
    return jax.shard_map(local, mesh=mesh, in_specs=in_specs, out_specs=out_specs, check_vma=False)
```

```python
import functools
import math

import jax
import jax.numpy as jnp
from jax import lax
from jax.experimental import pallas as pl
from jax.experimental.pallas import tpu as pltpu
from jax.sharding import PartitionSpec as P

HEADS = 9
KV_HEADS = 3
HEAD_DIM = 64
FF = 1536
REPEATS = HEADS // KV_HEADS
QW = HEADS * HEAD_DIM
KW = KV_HEADS * HEAD_DIM
EPSILON = 1e-05
ROPE_BASE = 100000.0
MASKED = -1e30
BOTH = ("dp", "fsdp")
F32 = jnp.float32
BF16 = jnp.bfloat16


def dot(a, b):
    return lax.dot_general(a, b, (((1,), (0,)), ((), ())), preferred_element_type=F32)


def dot_nt(a, b):
    return lax.dot_general(a, b, (((1,), (1,)), ((), ())), preferred_element_type=F32)


def dot_tn(a, b):
    return lax.dot_general(a, b, (((0,), (0,)), ((), ())), preferred_element_type=F32)


def params(mib=32):
    return pltpu.CompilerParams(vmem_limit_bytes=mib << 20)


def shape_of(shape, dtype):
    return jax.ShapeDtypeStruct(shape, dtype)


def cost(mega_flops, kilo_bytes):
    return pl.CostEstimate(
        flops=mega_flops * 1_000_000, bytes_accessed=kilo_bytes * 1000, transcendentals=0
    )


def whole(count):
    return [pl.BlockSpec(memory_space=pltpu.VMEM)] * count


def padded_rows(rows):
    return -(-(rows + 1) // 16) * 16


def padded_lanes(lanes):
    return -(-lanes // 128) * 128


def pack_attention(w_query, w_key_t, w_value_t, gain_one, gain_two):
    rows = w_query.shape[0]
    body = [w_query.astype(F32), w_key_t.astype(F32).T, w_value_t.astype(F32).T]
    used = sum(w.shape[1] for w in body)
    lanes = padded_lanes(used)
    body = jnp.concatenate(body + [jnp.zeros((rows, lanes - used), F32)], axis=1)
    gains = gain_lines(gain_one.astype(F32), gain_two.astype(F32), rows, lanes)
    return jnp.concatenate([body, gains], axis=0).astype(BF16)


def gain_lines(gain_one, gain_two, rows, lanes):
    spare = jnp.zeros((1, lanes - 2 * rows), F32)
    line = jnp.concatenate([gain_one, gain_two, spare], axis=1)
    return jnp.broadcast_to(line, (padded_rows(rows) - rows, lanes))


def pack_rest(w_gate, w_up, w_down_t, w_out):
    rows = w_gate.shape[0]
    turned = w_down_t.astype(F32)
    pieces = [turned[n * rows : (n + 1) * rows] for n in range(turned.shape[0] // rows)]
    body = [w_gate.astype(F32), w_up.astype(F32)] + pieces + [w_out.astype(F32)]
    return jnp.concatenate(body, axis=1).astype(BF16)


def unpack_attention(block, rows, q_cols, k_cols):
    ends = (0, q_cols, q_cols + k_cols, q_cols + 2 * k_cols)
    parts = [block[:rows, ends[n] : ends[n + 1]] for n in range(3)]
    gains = [block[rows : rows + 1, :rows], block[rows : rows + 1, rows : 2 * rows]]
    return [parts[0], parts[1].T, parts[2].T] + gains


def unpack_rest(block, lanes, down_shape):
    block = block.astype(F32)
    deep = down_shape[1]
    pieces = [block[:, n : n + deep] for n in range(2 * lanes, 3 * lanes, deep)]
    down = jnp.concatenate(pieces, axis=0)
    return [block[:, :lanes], block[:, lanes : 2 * lanes], down, block[:, 3 * lanes :]]


def pack_kernel(q, k, v, one, two, gate, up, down, o, attn_ref, rest_ref):
    attn_ref[...] = pack_attention(q[...], k[...], v[...], one[...], two[...])
    rest_ref[...] = pack_rest(gate[...], up[...], down[...], o[...])


def unpack_kernel(*refs):
    attn, rest = (
        r[0][...] + r[1][...].astype(F32) + r[2][...].astype(F32) + r[3][...].astype(F32)
        for r in (refs[:4], refs[4:8])
    )
    q, k, v, one, two, gate, up, down, o = refs[8:]
    parts = unpack_attention(attn, q.shape[0], q.shape[1], k.shape[0])
    parts += unpack_rest(rest, gate.shape[1], down.shape)
    for ref, part in zip((q, k, v, one, two, gate, up, down, o), parts, strict=True):
        ref[...] = part


def attention_rows(block_of, number, members, rows, q_cols, k_cols):
    blocks = [block_of(number * members + f).astype(F32) for f in range(members)]
    ends = (0, q_cols, q_cols + k_cols, q_cols + 2 * k_cols)
    spans = [b[:rows, ends[n] : ends[n + 1]] for n in range(3) for b in blocks]
    gains = (blocks[0][rows : rows + 1, :rows], blocks[0][rows : rows + 1, rows : 2 * rows])
    return jnp.concatenate(spans, axis=1), gains


def join_attention_kernel(members, rows, q_cols, k_cols, place_ref, *refs):
    halves, (wqkv_ref, one_ref, two_ref, blocks) = refs[:8], refs[8:]
    member, part = place_ref[0], place_ref[1]
    width = halves[0].shape[2]
    for core in range(2):
        for far in range(2):
            one, two = halves[4 * core + far], halves[4 * core + 2 + far]
            for near in range(2):
                for z in range(4):
                    other = (part ^ (2 * z + near)) * members + (member ^ (2 * far + core))
                    blocks[other, :, :width] = one[4 * near + z]
                    other = (part ^ (2 * z + far)) * members + (member ^ (2 * near + core))
                    blocks[other, :, width:] = two[4 * near + z]
    gains = []
    for pair in range(blocks.shape[0] // members // 2):
        made = [
            attention_rows(lambda n: blocks[n], 2 * pair + s, members, rows, q_cols, k_cols)
            for s in range(2)
        ]
        gains += [m[1] for m in made]
        span = slice(pair * 2 * rows, (pair + 1) * 2 * rows)
        wqkv_ref[span, :] = jnp.concatenate([m[0] for m in made], axis=0).astype(BF16)
    one_ref[...] = jnp.concatenate([g[0] for g in gains], axis=1)
    two_ref[...] = jnp.concatenate([g[1] for g in gains], axis=1)


def join_attention_plain(members, rows, q_cols, k_cols, gathered):
    parts = gathered.shape[0] // members
    made = [
        attention_rows(lambda n: gathered[n], s, members, rows, q_cols, k_cols)
        for s in range(parts)
    ]
    return (
        jnp.concatenate([m[0] for m in made], axis=0).astype(BF16),
        jnp.concatenate([m[1][0] for m in made], axis=1),
        jnp.concatenate([m[1][1] for m in made], axis=1),
    )


def join_rest_kernel(members, lanes, g_ref, gate_ref, up_ref, down_ref, wo_ref):
    rows = g_ref.shape[1]
    half = lanes // 2
    for pair in range(g_ref.shape[0] // members // 2):
        here = slice(pair * 2 * rows, (pair + 1) * 2 * rows)
        outs = []
        for f in range(members):
            first = 2 * pair * members + f
            a, b = (g_ref[n].astype(F32) for n in (first, first + members))
            cols = slice(f * lanes, (f + 1) * lanes)
            gate_ref[here, cols] = jnp.concatenate([a[:, :lanes], b[:, :lanes]], axis=0).astype(
                BF16
            )
            up_ref[here, cols] = jnp.concatenate(
                [a[:, lanes : 2 * lanes], b[:, lanes : 2 * lanes]], axis=0
            ).astype(BF16)
            outs.append(jnp.concatenate([a[:, 3 * lanes :], b[:, 3 * lanes :]], axis=0))
            a, b = a[:, 2 * lanes : 3 * lanes], b[:, 2 * lanes : 3 * lanes]
            top = jnp.concatenate([a[:, :half], b[:, :half]], axis=1)
            low = jnp.concatenate([a[:, half:], b[:, half:]], axis=1)
            down_ref[f * 2 * rows : (f + 1) * 2 * rows, pair * lanes : (pair + 1) * lanes] = (
                jnp.concatenate([top, low], axis=0).astype(BF16)
            )
        wo_ref[here, :] = jnp.concatenate(outs, axis=1).astype(BF16)


def join_rest_plain(members, lanes, gathered):
    rows = gathered.shape[1]
    parts = gathered.shape[0] // members
    width = rows * parts
    g = gathered.reshape(parts, members, rows, gathered.shape[2])
    deep = FF // parts

    def across(first, last):
        piece = g[..., first:last].transpose(0, 2, 1, 3)
        return piece.reshape(width, members * (last - first))

    down = g[..., 2 * lanes : 3 * lanes].reshape(parts, members, rows, lanes // deep, deep)
    down = down.transpose(1, 3, 2, 0, 4).reshape(width, FF)
    return across(0, lanes), across(lanes, 2 * lanes), down, across(3 * lanes, g.shape[3])


def after(value, *others):
    return lax.optimization_barrier((value, others))[0]


def swap(value, axis, bit):
    size = lax.axis_size(axis)
    return lax.ppermute(value, axis, [(n, n ^ bit) for n in range(size)])


def bundle_one_kernel(own, one, two, three, a_ref, b_ref):
    half = own.shape[1] // 2
    for n, ref in enumerate((own, one, two, three)):
        a_ref[n] = ref[:, :half]
        b_ref[n] = ref[:, half:]


def bundle_two_kernel(a, a_far, b, b_far, a_ref, b_ref):
    for out, parts in ((a_ref, (a, a_far)), (b_ref, (b, b_far))):
        for n, ref in enumerate(parts):
            out[n * 4 : (n + 1) * 4] = ref[...]


def gather_attention(block, early):
    rows, lanes = block.shape
    half = lanes // 2

    def bundled(kernel, count, *values):
        return pl.pallas_call(
            kernel,
            out_shape=(shape_of((count, rows, half), BF16),) * 2,
            in_specs=whole(4),
            out_specs=whole(2),
            compiler_params=params(),
            cost_estimate=cost(1, 1500),
            name="bundle",
        )(*values)

    along = [swap(block, "dp", 2 * n) for n in (1, 2, 3)]
    along, early = lax.optimization_barrier((along, early))
    a, b = bundled(bundle_one_kernel, 4, block, *along)
    a, b = bundled(bundle_two_kernel, 8, a, swap(a, "dp", 1), b, swap(b, "fsdp", 2))
    a_far, b_far = swap(a, "fsdp", 2), swap(b, "dp", 1)
    mine = (a, a_far, b, b_far)
    return mine + tuple(swap(value, "fsdp", 1) for value in mine), early


def add(a, b):
    return a.astype(F32) + b.astype(F32)


def reduce_one_kernel(a, a_got, b, b_got, a_keep, a_send, b_keep, b_send):
    for own, got, keep, send in ((a, a_got, a_keep, a_send), (b, b_got, b_keep, b_send)):
        keep[...] = add(own[0], got[0]).astype(BF16)
        send[...] = add(own[1], got[1]).astype(BF16)


def reduce_two_kernel(a, a_got, b, b_got, a_keep, a_send, b_keep, b_send):
    for own, got, keep, send in ((a, a_got, a_keep, a_send), (b, b_got, b_keep, b_send)):
        keep[...] = add(own[:4], got[:4]).astype(BF16)
        send[...] = add(own[4:], got[4:]).astype(BF16)


def reduce_three_kernel(a, a_got, b, b_got, own_ref, one, two, three):
    for n, ref in enumerate((own_ref, one, two, three)):
        made = jnp.concatenate([add(a[n], a_got[n]), add(b[n], b_got[n])], axis=1)
        ref[...] = made.astype(ref.dtype)


def reduce_call(kernel, count, values, out_types=(BF16,) * 4):
    rows = values[0].shape[-2]
    one, two = values[0].shape[-1], values[2].shape[-1]
    if count:
        shapes = [(count, rows, lanes) for lanes in (one, one, two, two)]
    else:
        shapes = [(rows, one + two)] * 4
    return pl.pallas_call(
        kernel,
        out_shape=[shape_of(s, t) for s, t in zip(shapes, out_types)],
        in_specs=whole(4),
        out_specs=whole(4),
        compiler_params=params(),
        cost_estimate=cost(1, 3000),
        name="reduce",
    )(*values)


def reduce_steps(a_keep, a_send, b_keep, b_send):
    got = yield (a_send, b_send), (swap(a_send, "fsdp", 1), swap(b_send, "fsdp", 1))
    values = (a_keep, got[0], b_keep, got[1])
    a_keep, a_send, b_keep, b_send = reduce_call(reduce_one_kernel, 8, values)
    got = yield (a_send, b_send), (swap(a_send, "fsdp", 2), swap(b_send, "dp", 1))
    values = (a_keep, got[0], b_keep, got[1])
    a_keep, a_send, b_keep, b_send = reduce_call(reduce_two_kernel, 4, values)
    got = yield (a_send, b_send), (swap(a_send, "dp", 1), swap(b_send, "fsdp", 2))
    values = (a_keep, got[0], b_keep, got[1])
    own, *send = reduce_call(reduce_three_kernel, 0, values, (F32, BF16, BF16, BF16))
    got = yield send, [swap(value, "dp", 2 * n) for n, value in zip((1, 2, 3), send)]
    yield [own] + list(got)


def reduce_all(made):
    steps = reduce_steps(*made)
    got = next(steps)[1]
    for _ in range(3):
        got = steps.send(got)[1]
    return steps.send(got)


def swap_halves(chunk):
    lane = lax.broadcasted_iota(jnp.int32, chunk.shape, 1)
    low = (lane % HEAD_DIM) < HEAD_DIM // 2
    return jnp.where(low, pltpu.roll(chunk, 96, 1), pltpu.roll(chunk, 32, 1))


def turn(vectors, cosine, sine):
    chunks = []
    for n in range(vectors.shape[1] // 128):
        chunk = vectors[:, n * 128 : (n + 1) * 128]
        chunks.append(chunk * cosine + swap_halves(chunk) * sine)
    return jnp.concatenate(chunks, axis=1)


def norm_scale(values):
    return lax.rsqrt(jnp.mean(values * values, axis=1, keepdims=True) + EPSILON)


def norm_back(inputs, scale, gain, grads):
    weighted = grads * gain
    term = jnp.sum(grads * (inputs * scale), axis=0, keepdims=True)
    cubed = scale * scale * scale
    mean = jnp.mean(weighted * inputs, axis=1, keepdims=True)
    return scale * weighted - inputs * (cubed * mean), term


def pre_kernel(x_ref, w_ref, gain_ref, cos_ref, sin_ref, q_ref, kv_ref):
    x = x_ref[...].astype(F32)
    normed = (x * norm_scale(x) * gain_ref[...]).astype(BF16)
    raw = dot(normed, w_ref[...])
    turned = turn(raw[:, : QW + KW], cos_ref[...], sin_ref[...])
    q_ref[...] = (turned[:, :QW].astype(BF16).astype(F32) * HEAD_DIM**-0.5).astype(BF16)
    kv_ref[...] = jnp.concatenate([turned[:, QW:], raw[:, QW + KW :]], axis=1).astype(BF16)


def row_range(lens_ref, micro, first_row, rows):
    end_zero = lens_ref[micro, 0]
    end_one = end_zero + lens_ref[micro, 1]
    end_two = end_one + lens_ref[micro, 2]
    places = first_row + lax.broadcasted_iota(jnp.int32, (1, rows), 1)

    def begin(at):
        return jnp.where(
            at < end_zero, 0, jnp.where(at < end_one, end_zero, jnp.where(at < end_two, end_one, at))
        )

    return places, begin(places), begin(first_row)


def mask_of(key_block, rows, places, begins):
    keys = key_block * rows + lax.broadcasted_iota(jnp.int32, (rows, rows), 0)
    bias = jnp.where((keys >= begins) & (keys <= places), 0.0, MASKED)
    return jnp.concatenate([bias] * REPEATS, axis=1)


def stacked(values, group):
    first = group * REPEATS
    return jnp.concatenate(
        [
            values[:, (first + n) * HEAD_DIM : (first + n + 1) * HEAD_DIM]
            for n in range(REPEATS)
        ],
        axis=0,
    )


def unstacked(groups):
    rows = groups[0].shape[0] // REPEATS
    return jnp.concatenate(
        [g[n * rows : (n + 1) * rows] for g in groups for n in range(REPEATS)], axis=1
    )


def head_of(values, number):
    return values[:, number * HEAD_DIM : (number + 1) * HEAD_DIM]


def place_kv(member, refs, kv):
    for distance, ref in enumerate(refs):
        kv[member ^ distance] = ref[...]


def forward_kernel(
    micro, lens_ref, place_ref, q_ref, kv_0, kv_1, kv_2, kv_3, out_ref, lse_ref, kv, acc, top, total
):
    rows = q_ref.shape[0]
    member = place_ref[0]
    places, begins, lowest = row_range(lens_ref, micro, member * rows, rows)
    place_kv(member, (kv_0, kv_1, kv_2, kv_3), kv)
    queries = [stacked(q_ref[...], g) for g in range(KV_HEADS)]
    acc[...] = jnp.zeros_like(acc)
    top[...] = jnp.full_like(top, MASKED)
    total[...] = jnp.zeros_like(total)

    def block(number, carry):
        bias = mask_of(number, rows, places, begins)
        both = kv[number]
        for g in range(KV_HEADS):
            keys, values = head_of(both, g), head_of(both, KV_HEADS + g)
            scores = dot_nt(keys, queries[g]) + bias
            before = top[g]
            now = jnp.maximum(before, jnp.max(scores, axis=0, keepdims=True))
            shrink = jnp.exp(before - now)
            weights = jnp.exp(scores - now)
            total[g] = total[g] * shrink + jnp.sum(weights, axis=0, keepdims=True)
            acc[g] = acc[g] * shrink + dot_tn(values, weights.astype(BF16))
            top[g] = now
        return carry

    lax.fori_loop(lowest // rows, member + 1, block, 0)
    done = []
    for g in range(KV_HEADS):
        done.append((acc[g] * (1.0 / total[g])).T)
        lse_ref[g] = top[g] + jnp.log(total[g])
    out_ref[...] = unstacked(done)


def backward_kernel(
    micro,
    lens_ref,
    place_ref,
    q_ref,
    kv_0,
    kv_1,
    kv_2,
    kv_3,
    out_ref,
    grad_ref,
    lse_ref,
    dq_ref,
    own_ref,
    far_ref,
    send_ref,
    kv,
    dkv,
    acc,
):
    rows = q_ref.shape[0]
    member = place_ref[0]
    places, begins, lowest = row_range(lens_ref, micro, member * rows, rows)
    place_kv(member, (kv_0, kv_1, kv_2, kv_3), kv)
    queries = [stacked(q_ref[...], g) for g in range(KV_HEADS)]
    grads = [stacked(grad_ref[...], g) for g in range(KV_HEADS)]
    product = grad_ref[...].astype(F32) * out_ref[...]
    dots = [jnp.sum(stacked(product, g).T, axis=0, keepdims=True) for g in range(KV_HEADS)]
    acc[...] = jnp.zeros_like(acc)
    dkv[...] = jnp.zeros_like(dkv)

    def block(number, carry):
        bias = mask_of(number, rows, places, begins)
        both = kv[number]
        grad_keys, grad_values = [], []
        for g in range(KV_HEADS):
            keys, values = head_of(both, g), head_of(both, KV_HEADS + g)
            probs = jnp.exp(dot_nt(keys, queries[g]) + bias - lse_ref[g])
            grad_probs = dot_nt(values, grads[g])
            grad_scores = (probs * (grad_probs - dots[g])).astype(BF16)
            grad_values.append(dot(probs.astype(BF16), grads[g]))
            grad_keys.append(dot(grad_scores, queries[g]))
            acc[g] = acc[g] + dot_tn(keys, grad_scores)
        dkv[number ^ member] = jnp.concatenate(grad_keys + grad_values, axis=1).astype(BF16)
        return carry

    lax.fori_loop(lowest // rows, member + 1, block, 0)
    dq_ref[...] = unstacked([acc[g].T for g in range(KV_HEADS)]) * HEAD_DIM**-0.5
    own_ref[...] = dkv[0]
    far_ref[...] = dkv[2]
    send_ref[0] = dkv[1]
    send_ref[1] = dkv[3]


def mid_kernel(
    members,
    parts,
    as_blocks,
    place_ref,
    x_ref,
    att_0,
    att_1,
    att_2,
    dy_ref,
    wo_ref,
    gate_ref,
    up_ref,
    down_ref,
    gain_ref,
    mixed_ref,
    dmid_ref,
    datt_ref,
    ggain_ref,
    *refs,
):
    grad_refs, held = refs[: len(refs) - 7], refs[len(refs) - 7 :]
    s_hidden, s_dgate, s_dup, s_branch, s_normed, s_dy, s_att = held
    step = pl.program_id(0)
    rows = x_ref.shape[0]
    here = pl.ds(pl.multiple_of(step * rows, rows), rows)
    gain = gain_ref[...]
    for n, ref in enumerate((att_0, att_1, att_2)):

        @pl.when(step == n)
        def _(ref=ref):
            s_att[here, :] = ref[...].astype(BF16)

    att = s_att[here, :]
    middle = x_ref[...].astype(F32) + dot(att, wo_ref[...])
    scale = norm_scale(middle)
    normed = (middle * scale * gain).astype(BF16)
    dy = dy_ref[...]
    out, dnormed = middle, 0.0
    for first in range(0, FF, FF // 2):
        cols = slice(first, first + FF // 2)
        gate = dot(normed, gate_ref[:, cols])
        up = dot(normed, up_ref[:, cols])
        sig = lax.logistic(gate)
        silu = gate * sig
        hidden = (silu * up).astype(BF16)
        s_hidden[here, cols] = hidden
        out = out + dot_nt(hidden, down_ref[:, cols])
        dhidden = dot(dy, down_ref[:, cols])
        dgate = (dhidden * up * sig * (1.0 + gate * (1.0 - sig))).astype(BF16)
        dup = (dhidden * silu).astype(BF16)
        s_dgate[here, cols] = dgate
        s_dup[here, cols] = dup
        dnormed = dnormed + dot_nt(dgate, gate_ref[:, cols]) + dot_nt(dup, up_ref[:, cols])
    mixed_ref[0] = out.T.astype(BF16)
    back, term = norm_back(middle, scale, gain, dnormed)
    dmid = dy.astype(F32) + back
    dmid_ref[...] = dmid
    branch = dmid.astype(BF16)
    datt_ref[...] = dot_nt(branch, wo_ref[...]).astype(BF16)
    s_branch[here, :] = branch
    s_normed[here, :] = normed
    s_dy[here, :] = dy

    @pl.when(step == 0)
    def _():
        ggain_ref[...] = term

    @pl.when(step > 0)
    def _():
        ggain_ref[...] += term

    @pl.when(step == pl.num_programs(0) - 1)
    def _():
        width = s_normed.shape[1]
        grad_out = dot_tn(s_att[...], s_branch[...])
        normed_t = s_normed[...].T
        dy_t = s_dy[...].T
        if not as_blocks:
            (full_ref,) = grad_refs
            full_ref[:, :FF] = dot(normed_t, s_dgate[...]).astype(BF16)
            full_ref[:, FF : 2 * FF] = dot(normed_t, s_dup[...]).astype(BF16)
            full_ref[:, 2 * FF : 3 * FF] = dot(dy_t, s_hidden[...]).astype(BF16)
            full_ref[:, 3 * FF :] = grad_out.astype(BF16)
            return
        a_keep, a_send, b_keep, b_send = grad_refs
        member, place = place_ref[0], place_ref[1]
        part = width // parts
        lanes = FF // members
        deep = FF // parts
        cols = width // members
        cut = a_keep.shape[3] - lanes
        for f in range(members):
            core, y = (member ^ f) & 1, (member ^ f) >> 1
            grad_gate = dot(normed_t, s_dgate[:, f * lanes : (f + 1) * lanes])
            grad_up = dot(normed_t, s_dup[:, f * lanes : (f + 1) * lanes])
            grad_down = dot(dy_t[f * cols : (f + 1) * cols], s_hidden[...])
            first, rest = [], []
            for n in range(parts):
                here = slice(n * part, (n + 1) * part)
                span = grad_down[:, n * deep : (n + 1) * deep]
                span = [span[i * part : (i + 1) * part] for i in range(cols // part)]
                span = [grad_up[here, cut:]] + span + [grad_out[here, f * cols : (f + 1) * cols]]
                pair = jnp.concatenate([grad_gate[here], grad_up[here, :cut]], axis=1)
                first.append(pair.astype(BF16))
                rest.append(jnp.concatenate(span, axis=1).astype(BF16))
            for side, a_ref, b_ref in ((0, a_keep, b_keep), (1, a_send, b_send)):

                @pl.when(core == side)
                def _(a_ref=a_ref, b_ref=b_ref, first=first, rest=rest, y=y):
                    for n in range(parts):
                        x, z = (place ^ n) & 1, (place ^ n) >> 1
                        a_ref[y, 4 * x + z] = first[n]
                        b_ref[x, 4 * y + z] = rest[n]


def blocks_of_rest(full, members, parts):
    width = full.shape[0]
    part, lanes, deep = width // parts, FF // members, FF // parts
    cols = width // members

    def across(first, last):
        piece = full[:, first:last].reshape(parts, part, members, (last - first) // members)
        return piece.transpose(0, 2, 1, 3)

    down = full[:, 2 * FF : 3 * FF].reshape(members, cols // part, part, parts, deep)
    down = down.transpose(3, 0, 2, 1, 4).reshape(parts, members, part, lanes)
    made = [across(0, FF), across(FF, 2 * FF), down, across(3 * FF, full.shape[1])]
    made = jnp.concatenate(made, axis=3)
    return made.reshape(parts * members, part, made.shape[3])


def post_kernel(
    x_ref,
    dq_ref,
    own_ref,
    near_ref,
    far_ref,
    dmid_ref,
    w_ref,
    gain_ref,
    cos_ref,
    sin_ref,
    *refs,
):
    dx_ref, raw_ref, normed_ref, term_ref = refs[len(refs) - 4 :]
    gain = gain_ref[...]
    x = x_ref[...].astype(F32)
    scale = norm_scale(x)
    normed_ref[...] = (x * scale * gain).astype(BF16)
    dkv = add(own_ref[...], near_ref[0]) + far_ref[...].astype(F32)
    turned = jnp.concatenate([dq_ref[...], dkv[:, :KW]], axis=1)
    turned = turn(turned, cos_ref[...], -sin_ref[...])
    raw = jnp.concatenate([turned, dkv[:, KW:]], axis=1).astype(BF16)
    raw_ref[...] = raw
    back, term = norm_back(x, scale, gain, dot_nt(raw, w_ref[...]))
    dx_ref[0] = (dmid_ref[...] + back).T
    term_ref[...] = term


def attention_blocks(grad_qkv, gain_one, gain_two, members, parts, store):
    width = grad_qkv.shape[0]
    part = width // parts
    q_cols, k_cols = QW // members, KW // members
    used = q_cols + 2 * k_cols
    lanes = padded_lanes(used)
    spare = jnp.zeros((part, lanes - used), F32)
    for n in range(parts):
        rows = slice(n * part, (n + 1) * part)
        gains = gain_lines(gain_one[:, rows], gain_two[:, rows], part, lanes)
        for f in range(members):
            spans = [
                grad_qkv[rows, f * q_cols : (f + 1) * q_cols],
                grad_qkv[rows, QW + f * k_cols : QW + (f + 1) * k_cols],
                grad_qkv[rows, QW + KW + f * k_cols : QW + KW + (f + 1) * k_cols],
                spare,
            ]
            body = jnp.concatenate(spans, axis=1)
            store(n, f, jnp.concatenate([body, gains], axis=0).astype(BF16))


def grads_kernel(members, parts, *refs):
    place_ref, raws, normeds, terms = refs[0], refs[1:4], refs[4:7], refs[7:10]
    gain_two_ref, outs = refs[10], refs[11:]
    raw = jnp.concatenate([r[...] for r in raws], axis=0)
    normed = jnp.concatenate([r[...] for r in normeds], axis=0)
    grad_qkv = dot_tn(normed, raw)
    gain_one = terms[0][...] + terms[1][...] + terms[2][...]
    if len(outs) == 2:
        outs[0][...] = grad_qkv
        outs[1][...] = gain_one
        return
    a_keep, a_send, b_keep, b_send, s_a, s_b = outs
    member, place = place_ref[0], place_ref[1]
    half = s_a.shape[4]

    def store(n, f, block):
        away = place ^ n
        x, z = away & 1, away >> 1
        away = member ^ f
        core, y = away & 1, away >> 1
        s_a[core, y, 4 * x + z] = block[:, :half]
        s_b[core, x, 4 * y + z] = block[:, half:]

    attention_blocks(grad_qkv, gain_one, gain_two_ref[...], members, parts, store)
    a_keep[...] = s_a[0]
    a_send[...] = s_a[1]
    b_keep[...] = s_b[0]
    b_send[...] = s_b[1]


def local(
    tokens,
    cotangent,
    lengths,
    gain_attn,
    w_query,
    w_key,
    w_value,
    w_out,
    gain_mlp,
    w_gate,
    w_up,
    w_down,
):
    members = lax.axis_size("fsdp")
    parts = lax.axis_size("dp")
    count = parts * members
    member = lax.axis_index("fsdp")
    micro, rows, width = tokens.shape
    every = micro * rows
    part = w_query.shape[0]
    q_cols, k_cols = w_query.shape[1], w_key.shape[1]
    lanes = w_gate.shape[1]
    deep = padded_rows(part)
    attn_lanes = padded_lanes(q_cols + 2 * k_cols)
    rest_lanes = 3 * lanes + w_out.shape[1]
    as_blocks = parts == 8 and part % 8 == 0 and width // members == 2 * part

    lens = lengths[:, 0, :]
    place = jnp.stack([member, lax.axis_index("dp")]).astype(jnp.int32)
    ends = jnp.cumsum(lens, axis=1)
    at = member * rows + lax.broadcasted_iota(jnp.int32, (micro, rows), 1)
    begins = jnp.zeros_like(at)
    for n in range(lens.shape[1]):
        following = ends[:, n : n + 1] if n < lens.shape[1] - 1 else at
        begins = jnp.where(ends[:, n : n + 1] <= at, following, begins)
    posit = (at - begins).reshape(every, 1).astype(F32)
    lane = lax.broadcasted_iota(jnp.int32, (1, 128), 1)
    halfway = HEAD_DIM // 2
    freqs = jnp.exp((lane % halfway).astype(F32) * (-math.log(ROPE_BASE) / halfway))
    angles = posit * freqs
    cosine = jnp.cos(angles)
    sine = jnp.sin(angles) * jnp.where(lane % HEAD_DIM < halfway, -1.0, 1.0)

    gain_rows = (gain_attn.reshape(1, part), gain_mlp.reshape(1, part))
    own = (w_query, w_key.T, w_value.T) + gain_rows
    others = (w_gate, w_up, w_down.T, w_out)
    if as_blocks:
        attn_block, rest_block = pl.pallas_call(
            pack_kernel,
            out_shape=(
                shape_of((deep, attn_lanes), BF16),
                shape_of((part, rest_lanes), BF16),
            ),
            in_specs=whole(9),
            out_specs=whole(2),
            compiler_params=params(56),
            cost_estimate=cost(1, 500),
            name="pack",
        )(*own, *others)
    else:
        attn_block, rest_block = pack_attention(*own), pack_rest(*others)
    rest_all = lax.all_gather(rest_block, BOTH, axis=0, tiled=False)
    smem = pl.BlockSpec(memory_space=pltpu.SMEM)
    x = tokens.reshape(every, width)
    dy = cotangent.reshape(every, width)
    if as_blocks:
        gathered, early = gather_attention(attn_block, (cosine, sine, x))
        cosine, sine, x = early
        wqkv, gain_one, gain_two = pl.pallas_call(
            functools.partial(join_attention_kernel, members, part, q_cols, k_cols),
            out_shape=(
                shape_of((width, QW + 2 * KW), BF16),
                shape_of((1, width), F32),
                shape_of((1, width), F32),
            ),
            in_specs=[smem] + whole(8),
            out_specs=whole(3),
            scratch_shapes=[pltpu.VMEM((count, deep, attn_lanes), BF16)],
            compiler_params=params(56),
            cost_estimate=cost(10, 6000),
            name="join_attention",
        )(place, *gathered)
        gate_w, up_w, down_w, wo = pl.pallas_call(
            functools.partial(join_rest_kernel, members, lanes),
            out_shape=(shape_of((width, FF), BF16),) * 3 + (shape_of((QW, width), BF16),),
            in_specs=whole(1),
            out_specs=whole(4),
            compiler_params=params(),
            cost_estimate=cost(10, 14000),
            name="join_rest",
        )(rest_all)
    else:
        attn_all = lax.all_gather(attn_block, BOTH, axis=0, tiled=False)
        wqkv, gain_one, gain_two = join_attention_plain(members, part, q_cols, k_cols, attn_all)
        gate_w, up_w, down_w, wo = join_rest_plain(members, lanes, rest_all)

    def by_rows(cols):
        return pl.BlockSpec((rows, cols), lambda n: (n, 0))

    def same(*shape):
        return pl.BlockSpec(shape, lambda n: (0,) * len(shape))

    def once(*shape):
        return pl.BlockSpec(
            shape, lambda n: (0,) * len(shape), pipeline_mode=pl.Buffered(buffer_count=1)
        )

    def only(number, cols):
        return pl.BlockSpec((rows, cols), lambda n: (number, 0))

    def turned(number):
        return pl.BlockSpec((1, width, rows), lambda n: (number, 0, 0))

    held = pltpu.VMEM((KV_HEADS, HEAD_DIM, REPEATS * rows), F32)
    line = (KV_HEADS, 1, REPEATS * rows)
    kv_blocks = pltpu.VMEM((members, rows, 2 * KW), BF16)
    kv_block = same(rows, 2 * KW)
    outward = [(0, 2), (1, 3)]
    queries, sent = [], []
    for m in range(micro):
        query, kv = pl.pallas_call(
            pre_kernel,
            grid=(1,),
            out_shape=(shape_of((rows, QW), BF16), shape_of((rows, 2 * KW), BF16)),
            in_specs=[
                only(m, width),
                same(width, QW + 2 * KW),
                same(1, width),
                only(m, 128),
                only(m, 128),
            ],
            out_specs=(same(rows, QW), same(rows, 2 * KW)),
            compiler_params=params(),
            cost_estimate=cost(500, 6000),
            name="pre",
        )(x, wqkv, gain_one, cosine, sine)
        queries.append(query)
        sent.append((kv, swap(kv, "fsdp", 1), lax.ppermute(kv, "fsdp", outward)))

    kvs, attended, logsums = [], [], []
    for m in range(micro):
        far = after(sent[m][2], *attended[-1:])
        kvs.append(sent[m][:2] + (far, swap(far, "fsdp", 1)))
        out, logsum = pl.pallas_call(
            functools.partial(forward_kernel, m),
            grid=(1,),
            out_shape=(shape_of((rows, QW), F32), shape_of(line, F32)),
            in_specs=[smem, smem, same(rows, QW)] + [kv_block] * 4,
            out_specs=(same(rows, QW), same(*line)),
            scratch_shapes=[kv_blocks, held, pltpu.VMEM(line, F32), pltpu.VMEM(line, F32)],
            compiler_params=params(),
            cost_estimate=cost(8000, 4000),
            name="attend_forward",
        )(lens, place, queries[m], *kvs[m])
        attended.append(out)
        logsums.append(logsum)

    if as_blocks:
        cut = rest_lanes // 256 * 128
        halves = (cut, cut, rest_lanes - cut, rest_lanes - cut)
        grad_shapes = [(2, 8, part, lane_count) for lane_count in halves]
    else:
        grad_shapes = [(width, 3 * FF + width)]
    mixed, dmid, datt, grad_two, *grad_rest = pl.pallas_call(
        functools.partial(mid_kernel, members, parts, as_blocks),
        grid=(micro,),
        out_shape=[
            shape_of((micro, width, rows), BF16),
            shape_of((every, width), F32),
            shape_of((every, QW), BF16),
            shape_of((1, width), F32),
        ]
        + [shape_of(s, BF16) for s in grad_shapes],
        in_specs=[smem, by_rows(width)]
        + [once(rows, QW)] * 3
        + [
            by_rows(width),
            once(QW, width),
            once(width, FF),
            once(width, FF),
            once(width, FF),
            once(1, width),
        ],
        out_specs=[
            pl.BlockSpec((1, width, rows), lambda n: (n, 0, 0)),
            by_rows(width),
            by_rows(QW),
            same(1, width),
        ]
        + [once(*s) for s in grad_shapes],
        scratch_shapes=[
            pltpu.VMEM((every, FF), BF16),
            pltpu.VMEM((every, FF), BF16),
            pltpu.VMEM((every, FF), BF16),
            pltpu.VMEM((every, width), BF16),
            pltpu.VMEM((every, width), BF16),
            pltpu.VMEM((every, width), BF16),
            pltpu.VMEM((every, QW), BF16),
        ],
        compiler_params=params(60),
        cost_estimate=cost(40000, 40000),
        name="mid",
    )(place, x, *attended, dy, wo, gate_w, up_w, down_w, gain_two)

    if as_blocks:
        steps = reduce_steps(*grad_rest)
        got = next(steps)[1]
    else:
        grad_rest = blocks_of_rest(grad_rest[0], members, parts)
        rest_sum = lax.psum_scatter(grad_rest, BOTH, scatter_dimension=0, tiled=False)

    back = []
    for m in range(micro):
        query = queries[m]
        if m == 1 and as_blocks:
            send, got = steps.send([after(value, back[0][0]) for value in got])
            query = after(query, *send)
        if m == 2:
            query = after(query, back[0][3])
        dq, keep, far, send = pl.pallas_call(
            functools.partial(backward_kernel, m),
            grid=(1,),
            out_shape=(
                shape_of((rows, QW), F32),
                shape_of((rows, 2 * KW), BF16),
                shape_of((rows, 2 * KW), BF16),
                shape_of((2, rows, 2 * KW), BF16),
            ),
            in_specs=[smem, smem, same(rows, QW)]
            + [kv_block] * 4
            + [same(rows, QW), only(m, QW), same(*line)],
            out_specs=(same(rows, QW), kv_block, kv_block, same(2, rows, 2 * KW)),
            scratch_shapes=[kv_blocks, kv_blocks, held],
            compiler_params=params(),
            cost_estimate=cost(11000, 5000),
            name="attend_backward",
        )(lens, place, query, *kvs[m], attended[m], datt, logsums[m])
        near = swap(send, "fsdp", 1)
        far = add(far, near[1]).astype(BF16)
        back.append((dq, keep, near, far))
    inward = [(b, a) for a, b in outward]
    if as_blocks:
        got = steps.send([after(value, back[-1][0]) for value in got])[1]

    input_grad = ()
    raws, normeds, terms = [], [], []
    for m in range(micro):
        dq, keep, near, far = back[m]
        far = lax.ppermute(far, "fsdp", inward)
        if m == 2 and as_blocks:
            send, got = steps.send([after(value, raws[-1]) for value in got])
            dq = after(dq, *send)
        made, raw, normed, term = pl.pallas_call(
            post_kernel,
            grid=(1,),
            out_shape=(
                shape_of((micro, width, rows), F32),
                shape_of((rows, QW + 2 * KW), BF16),
                shape_of((rows, width), BF16),
                shape_of((1, width), F32),
            ),
            in_specs=[
                only(m, width),
                same(rows, QW),
                kv_block,
                pl.BlockSpec((1, rows, 2 * KW), lambda n: (0, 0, 0)),
                kv_block,
                only(m, width),
                same(width, QW + 2 * KW),
                same(1, width),
                only(m, 128),
                only(m, 128),
            ]
            + [pl.BlockSpec(memory_space=pl.ANY)] * len(input_grad),
            out_specs=(
                turned(m),
                same(rows, QW + 2 * KW),
                same(rows, width),
                same(1, width),
            ),
            input_output_aliases={10: 0} if input_grad else {},
            compiler_params=params(),
            cost_estimate=cost(2000, 8000),
            name="post",
        )(x, dq, keep, near, far, dmid, wqkv, gain_one, cosine, sine, *input_grad)
        input_grad = (made,)
        raws.append(raw)
        normeds.append(normed)
        terms.append(term)

    if as_blocks:
        made = (shape_of((2, 8, deep, attn_lanes // 2), BF16),) * 4
        scratch = [pltpu.VMEM((2, 2, 8, deep, attn_lanes // 2), BF16)] * 2
    else:
        made = (shape_of((width, QW + 2 * KW), F32), shape_of((1, width), F32))
        scratch = []
    made = pl.pallas_call(
        functools.partial(grads_kernel, members, parts),
        out_shape=made,
        in_specs=[smem] + whole(10),
        out_specs=whole(len(made)),
        scratch_shapes=scratch,
        compiler_params=params(),
        cost_estimate=cost(3000, 8000),
        name="grads",
    )(place, *raws, *normeds, *terms, grad_two)

    if as_blocks:
        rest_sum = steps.send(got)
        shapes = [
            (part, q_cols),
            (k_cols, part),
            (k_cols, part),
            (1, part),
            (1, part),
            w_gate.shape,
            w_up.shape,
            w_down.shape[::-1],
            w_out.shape,
        ]
        grads = pl.pallas_call(
            unpack_kernel,
            out_shape=tuple(shape_of(s, F32) for s in shapes),
            in_specs=whole(8),
            out_specs=whole(9),
            compiler_params=params(),
            cost_estimate=cost(1, 3000),
            name="unpack",
        )(*reduce_all(made), *rest_sum)
    else:
        blocks = []
        attention_blocks(
            made[0], made[1], grad_two, members, parts, lambda n, f, block: blocks.append(block)
        )
        attn_sum = lax.psum_scatter(
            jnp.stack(blocks), BOTH, scatter_dimension=0, tiled=False
        ).astype(F32)
        grads = unpack_attention(attn_sum, part, q_cols, k_cols)
        grads += unpack_rest(rest_sum, lanes, w_down.shape[::-1])
    g_query, g_key, g_value, g_one, g_two, g_gate, g_up, g_down, g_out = grads
    return (
        mixed.transpose(0, 2, 1),
        input_grad[0].transpose(0, 2, 1),
        g_one.reshape(-1),
        g_query,
        g_key.T,
        g_value.T,
        g_out,
        g_two.reshape(-1),
        g_gate,
        g_up,
        g_down.T,
    )


def solution(mesh):
    rows = P(None, BOTH, None)
    block = P(*BOTH)
    gain = P("dp")
    in_specs = (rows, rows, P(None, "dp", None), gain)
    in_specs += (block, block, block, block, gain, block, block, block)
    out_specs = (rows, rows, gain, block, block, block, block, gain, block, block, block)
    return jax.shard_map(local, mesh=mesh, in_specs=in_specs, out_specs=out_specs, check_vma=False)
```

```python
import functools
import math

import jax
import jax.numpy as jnp
from jax import lax
from jax.experimental import pallas as pl
from jax.experimental.pallas import tpu as pltpu
from jax.sharding import PartitionSpec as P

HEADS = 9
KV_HEADS = 3
HEAD_DIM = 64
FF = 1536
REPEATS = HEADS // KV_HEADS
QW = HEADS * HEAD_DIM
KW = KV_HEADS * HEAD_DIM
EPSILON = 1e-05
ROPE_BASE = 100000.0
MASKED = -1e30
BOTH = ("dp", "fsdp")
F32 = jnp.float32
BF16 = jnp.bfloat16


def dot(a, b):
    return lax.dot_general(a, b, (((1,), (0,)), ((), ())), preferred_element_type=F32)


def dot_nt(a, b):
    return lax.dot_general(a, b, (((1,), (1,)), ((), ())), preferred_element_type=F32)


def dot_tn(a, b):
    return lax.dot_general(a, b, (((0,), (0,)), ((), ())), preferred_element_type=F32)


def params(mib=32):
    return pltpu.CompilerParams(vmem_limit_bytes=mib << 20)


def shape_of(shape, dtype):
    return jax.ShapeDtypeStruct(shape, dtype)


def cost(mega_flops, kilo_bytes):
    return pl.CostEstimate(
        flops=mega_flops * 1_000_000, bytes_accessed=kilo_bytes * 1000, transcendentals=0
    )


def whole(count):
    return [pl.BlockSpec(memory_space=pltpu.VMEM)] * count


def padded_rows(rows):
    return -(-(rows + 1) // 16) * 16


def padded_lanes(lanes):
    return -(-lanes // 128) * 128


def pack_attention(w_query, w_key_t, w_value_t, gain_one, gain_two):
    rows = w_query.shape[0]
    body = [w_query.astype(F32), w_key_t.astype(F32).T, w_value_t.astype(F32).T]
    used = sum(w.shape[1] for w in body)
    lanes = padded_lanes(used)
    body = jnp.concatenate(body + [jnp.zeros((rows, lanes - used), F32)], axis=1)
    gains = gain_lines(gain_one.astype(F32), gain_two.astype(F32), rows, lanes)
    return jnp.concatenate([body, gains], axis=0).astype(BF16)


def gain_lines(gain_one, gain_two, rows, lanes):
    spare = jnp.zeros((1, lanes - 2 * rows), F32)
    line = jnp.concatenate([gain_one, gain_two, spare], axis=1)
    return jnp.broadcast_to(line, (padded_rows(rows) - rows, lanes))


def pack_rest(w_gate, w_up, w_down_t, w_out):
    rows = w_gate.shape[0]
    turned = w_down_t.astype(F32)
    pieces = [turned[n * rows : (n + 1) * rows] for n in range(turned.shape[0] // rows)]
    body = [w_gate.astype(F32), w_up.astype(F32)] + pieces + [w_out.astype(F32)]
    return jnp.concatenate(body, axis=1).astype(BF16)


def unpack_attention(block, rows, q_cols, k_cols):
    ends = (0, q_cols, q_cols + k_cols, q_cols + 2 * k_cols)
    parts = [block[:rows, ends[n] : ends[n + 1]] for n in range(3)]
    gains = [block[rows : rows + 1, :rows], block[rows : rows + 1, rows : 2 * rows]]
    return [parts[0], parts[1].T, parts[2].T] + gains


def unpack_rest(block, lanes, down_shape):
    block = block.astype(F32)
    deep = down_shape[1]
    pieces = [block[:, n : n + deep] for n in range(2 * lanes, 3 * lanes, deep)]
    down = jnp.concatenate(pieces, axis=0)
    return [block[:, :lanes], block[:, lanes : 2 * lanes], down, block[:, 3 * lanes :]]


def pack_kernel(q, k, v, one, two, gate, up, down, o, attn_ref, rest_ref):
    attn_ref[...] = pack_attention(q[...], k[...], v[...], one[...], two[...])
    rest_ref[...] = pack_rest(gate[...], up[...], down[...], o[...])


def unpack_kernel(*refs):
    attn, rest = (
        r[0][...] + r[1][...].astype(F32) + r[2][...].astype(F32) + r[3][...].astype(F32)
        for r in (refs[:4], refs[4:8])
    )
    q, k, v, one, two, gate, up, down, o = refs[8:]
    parts = unpack_attention(attn, q.shape[0], q.shape[1], k.shape[0])
    parts += unpack_rest(rest, gate.shape[1], down.shape)
    for ref, part in zip((q, k, v, one, two, gate, up, down, o), parts, strict=True):
        ref[...] = part


def attention_rows(block_of, number, members, rows, q_cols, k_cols):
    blocks = [block_of(number * members + f).astype(F32) for f in range(members)]
    ends = (0, q_cols, q_cols + k_cols, q_cols + 2 * k_cols)
    spans = [b[:rows, ends[n] : ends[n + 1]] for n in range(3) for b in blocks]
    gains = (blocks[0][rows : rows + 1, :rows], blocks[0][rows : rows + 1, rows : 2 * rows])
    return jnp.concatenate(spans, axis=1), gains


def join_attention_kernel(members, rows, q_cols, k_cols, place_ref, *refs):
    halves, (wqkv_ref, one_ref, two_ref, blocks) = refs[:8], refs[8:]
    member, part = place_ref[0], place_ref[1]
    width = halves[0].shape[2]
    for core in range(2):
        for far in range(2):
            one, two = halves[4 * core + far], halves[4 * core + 2 + far]
            for near in range(2):
                for z in range(4):
                    other = (part ^ (2 * z + near)) * members + (member ^ (2 * far + core))
                    blocks[other, :, :width] = one[4 * near + z]
                    other = (part ^ (2 * z + far)) * members + (member ^ (2 * near + core))
                    blocks[other, :, width:] = two[4 * near + z]
    gains = []
    for pair in range(blocks.shape[0] // members // 2):
        made = [
            attention_rows(lambda n: blocks[n], 2 * pair + s, members, rows, q_cols, k_cols)
            for s in range(2)
        ]
        gains += [m[1] for m in made]
        span = slice(pair * 2 * rows, (pair + 1) * 2 * rows)
        wqkv_ref[span, :] = jnp.concatenate([m[0] for m in made], axis=0).astype(BF16)
    one_ref[...] = jnp.concatenate([g[0] for g in gains], axis=1)
    two_ref[...] = jnp.concatenate([g[1] for g in gains], axis=1)


def join_attention_plain(members, rows, q_cols, k_cols, gathered):
    parts = gathered.shape[0] // members
    made = [
        attention_rows(lambda n: gathered[n], s, members, rows, q_cols, k_cols)
        for s in range(parts)
    ]
    return (
        jnp.concatenate([m[0] for m in made], axis=0).astype(BF16),
        jnp.concatenate([m[1][0] for m in made], axis=1),
        jnp.concatenate([m[1][1] for m in made], axis=1),
    )


def join_rest_kernel(members, lanes, g_ref, gate_ref, up_ref, down_ref, wo_ref):
    rows = g_ref.shape[1]
    half = lanes // 2
    for pair in range(g_ref.shape[0] // members // 2):
        here = slice(pair * 2 * rows, (pair + 1) * 2 * rows)
        outs = []
        for f in range(members):
            first = 2 * pair * members + f
            a, b = (g_ref[n].astype(F32) for n in (first, first + members))
            cols = slice(f * lanes, (f + 1) * lanes)
            gate_ref[here, cols] = jnp.concatenate([a[:, :lanes], b[:, :lanes]], axis=0).astype(
                BF16
            )
            up_ref[here, cols] = jnp.concatenate(
                [a[:, lanes : 2 * lanes], b[:, lanes : 2 * lanes]], axis=0
            ).astype(BF16)
            outs.append(jnp.concatenate([a[:, 3 * lanes :], b[:, 3 * lanes :]], axis=0))
            a, b = a[:, 2 * lanes : 3 * lanes], b[:, 2 * lanes : 3 * lanes]
            top = jnp.concatenate([a[:, :half], b[:, :half]], axis=1)
            low = jnp.concatenate([a[:, half:], b[:, half:]], axis=1)
            down_ref[f * 2 * rows : (f + 1) * 2 * rows, pair * lanes : (pair + 1) * lanes] = (
                jnp.concatenate([top, low], axis=0).astype(BF16)
            )
        wo_ref[here, :] = jnp.concatenate(outs, axis=1).astype(BF16)


def join_rest_plain(members, lanes, gathered):
    rows = gathered.shape[1]
    parts = gathered.shape[0] // members
    width = rows * parts
    g = gathered.reshape(parts, members, rows, gathered.shape[2])
    deep = FF // parts

    def across(first, last):
        piece = g[..., first:last].transpose(0, 2, 1, 3)
        return piece.reshape(width, members * (last - first))

    down = g[..., 2 * lanes : 3 * lanes].reshape(parts, members, rows, lanes // deep, deep)
    down = down.transpose(1, 3, 2, 0, 4).reshape(width, FF)
    return across(0, lanes), across(lanes, 2 * lanes), down, across(3 * lanes, g.shape[3])


def after(value, *others):
    return lax.optimization_barrier((value, others))[0]


def swap(value, axis, bit):
    size = lax.axis_size(axis)
    return lax.ppermute(value, axis, [(n, n ^ bit) for n in range(size)])


def bundle_one_kernel(own, one, two, three, a_ref, b_ref):
    half = own.shape[1] // 2
    for n, ref in enumerate((own, one, two, three)):
        a_ref[n] = ref[:, :half]
        b_ref[n] = ref[:, half:]


def bundle_two_kernel(a, a_far, b, b_far, a_ref, b_ref):
    for out, parts in ((a_ref, (a, a_far)), (b_ref, (b, b_far))):
        for n, ref in enumerate(parts):
            out[n * 4 : (n + 1) * 4] = ref[...]


def gather_attention(block, early):
    rows, lanes = block.shape
    half = lanes // 2

    def bundled(kernel, count, *values):
        return pl.pallas_call(
            kernel,
            out_shape=(shape_of((count, rows, half), BF16),) * 2,
            in_specs=whole(4),
            out_specs=whole(2),
            compiler_params=params(),
            cost_estimate=cost(1, 1500),
            name="bundle",
        )(*values)

    along = [swap(block, "dp", 2 * n) for n in (1, 2, 3)]
    along, early = lax.optimization_barrier((along, early))
    a, b = bundled(bundle_one_kernel, 4, block, *along)
    a, b = bundled(bundle_two_kernel, 8, a, swap(a, "dp", 1), b, swap(b, "fsdp", 2))
    a_far, b_far = swap(a, "fsdp", 2), swap(b, "dp", 1)
    mine = (a, a_far, b, b_far)
    return mine + tuple(swap(value, "fsdp", 1) for value in mine), early


def add(a, b):
    return a.astype(F32) + b.astype(F32)


def reduce_one_kernel(a, a_got, b, b_got, a_keep, a_send, b_keep, b_send):
    for own, got, keep, send in ((a, a_got, a_keep, a_send), (b, b_got, b_keep, b_send)):
        keep[...] = add(own[0], got[0]).astype(BF16)
        send[...] = add(own[1], got[1]).astype(BF16)


def reduce_two_kernel(a, a_got, b, b_got, a_keep, a_send, b_keep, b_send):
    for own, got, keep, send in ((a, a_got, a_keep, a_send), (b, b_got, b_keep, b_send)):
        keep[...] = add(own[:4], got[:4]).astype(BF16)
        send[...] = add(own[4:], got[4:]).astype(BF16)


def reduce_three_kernel(a, a_got, b, b_got, own_ref, one, two, three):
    for n, ref in enumerate((own_ref, one, two, three)):
        made = jnp.concatenate([add(a[n], a_got[n]), add(b[n], b_got[n])], axis=1)
        ref[...] = made.astype(ref.dtype)


def reduce_call(kernel, count, values, out_types=(BF16,) * 4):
    rows = values[0].shape[-2]
    one, two = values[0].shape[-1], values[2].shape[-1]
    if count:
        shapes = [(count, rows, lanes) for lanes in (one, one, two, two)]
    else:
        shapes = [(rows, one + two)] * 4
    return pl.pallas_call(
        kernel,
        out_shape=[shape_of(s, t) for s, t in zip(shapes, out_types)],
        in_specs=whole(4),
        out_specs=whole(4),
        compiler_params=params(),
        cost_estimate=cost(1, 3000),
        name="reduce",
    )(*values)


def reduce_steps(a_keep, a_send, b_keep, b_send):
    got = yield (a_send, b_send), (swap(a_send, "fsdp", 1), swap(b_send, "fsdp", 1))
    values = (a_keep, got[0], b_keep, got[1])
    a_keep, a_send, b_keep, b_send = reduce_call(reduce_one_kernel, 8, values)
    got = yield (a_send, b_send), (swap(a_send, "fsdp", 2), swap(b_send, "dp", 1))
    values = (a_keep, got[0], b_keep, got[1])
    a_keep, a_send, b_keep, b_send = reduce_call(reduce_two_kernel, 4, values)
    got = yield (a_send, b_send), (swap(a_send, "dp", 1), swap(b_send, "fsdp", 2))
    values = (a_keep, got[0], b_keep, got[1])
    own, *send = reduce_call(reduce_three_kernel, 0, values, (F32, BF16, BF16, BF16))
    got = yield send, [swap(value, "dp", 2 * n) for n, value in zip((1, 2, 3), send)]
    yield [own] + list(got)


def reduce_all(made):
    steps = reduce_steps(*made)
    got = next(steps)[1]
    for _ in range(3):
        got = steps.send(got)[1]
    return steps.send(got)


def swap_halves(chunk):
    lane = lax.broadcasted_iota(jnp.int32, chunk.shape, 1)
    low = (lane % HEAD_DIM) < HEAD_DIM // 2
    return jnp.where(low, pltpu.roll(chunk, 96, 1), pltpu.roll(chunk, 32, 1))


def turn(vectors, cosine, sine):
    chunks = []
    for n in range(vectors.shape[1] // 128):
        chunk = vectors[:, n * 128 : (n + 1) * 128]
        chunks.append(chunk * cosine + swap_halves(chunk) * sine)
    return jnp.concatenate(chunks, axis=1)


def norm_scale(values):
    return lax.rsqrt(jnp.mean(values * values, axis=1, keepdims=True) + EPSILON)


def norm_back(inputs, scale, gain, grads):
    weighted = grads * gain
    term = jnp.sum(grads * (inputs * scale), axis=0, keepdims=True)
    cubed = scale * scale * scale
    mean = jnp.mean(weighted * inputs, axis=1, keepdims=True)
    return scale * weighted - inputs * (cubed * mean), term


def pre_kernel(x_ref, w_ref, gain_ref, cos_ref, sin_ref, q_ref, kv_ref):
    x = x_ref[...].astype(F32)
    normed = (x * norm_scale(x) * gain_ref[...]).astype(BF16)
    raw = dot(normed, w_ref[...])
    turned = turn(raw[:, : QW + KW], cos_ref[...], sin_ref[...])
    q_ref[...] = (turned[:, :QW].astype(BF16).astype(F32) * HEAD_DIM**-0.5).astype(BF16)
    kv_ref[...] = jnp.concatenate([turned[:, QW:], raw[:, QW + KW :]], axis=1).astype(BF16)


def row_range(lens_ref, micro, first_row, rows):
    end_zero = lens_ref[micro, 0]
    end_one = end_zero + lens_ref[micro, 1]
    end_two = end_one + lens_ref[micro, 2]
    places = first_row + lax.broadcasted_iota(jnp.int32, (1, rows), 1)

    def begin(at):
        return jnp.where(
            at < end_zero, 0, jnp.where(at < end_one, end_zero, jnp.where(at < end_two, end_one, at))
        )

    return places, begin(places), begin(first_row)


def mask_of(key_block, rows, places, begins):
    keys = key_block * rows + lax.broadcasted_iota(jnp.int32, (rows, rows), 0)
    bias = jnp.where((keys >= begins) & (keys <= places), 0.0, MASKED)
    return jnp.concatenate([bias] * REPEATS, axis=1)


def diagonal_mask(start, first, rows, places, begins):
    keys = start + lax.broadcasted_iota(jnp.int32, (first[1] - first[0], rows - first[0]), 0)
    allowed = (keys >= begins[:, first[0] :]) & (keys <= places[:, first[0] :])
    return jnp.concatenate([jnp.where(allowed, 0.0, MASKED)] * REPEATS, axis=1)


def spans_from(first, rows):
    return [slice(n * rows + first, (n + 1) * rows) for n in range(REPEATS)]


def lanes_from(value, first, rows):
    return jnp.concatenate([value[:, span] for span in spans_from(first, rows)], axis=1)


def rows_from(value, first, rows):
    return jnp.concatenate([value[span] for span in spans_from(first, rows)], axis=0)


def put_lanes(ref, group, value, first, rows):
    for n, span in enumerate(spans_from(first, rows)):
        ref[group, :, span] = value[:, n * (rows - first) : (n + 1) * (rows - first)]


def stacked(values, group):
    first = group * REPEATS
    return jnp.concatenate(
        [
            values[:, (first + n) * HEAD_DIM : (first + n + 1) * HEAD_DIM]
            for n in range(REPEATS)
        ],
        axis=0,
    )


def unstacked(groups):
    rows = groups[0].shape[0] // REPEATS
    return jnp.concatenate(
        [g[n * rows : (n + 1) * rows] for g in groups for n in range(REPEATS)], axis=1
    )


def head_of(values, number):
    return values[:, number * HEAD_DIM : (number + 1) * HEAD_DIM]


def place_kv(member, refs, kv):
    for distance, ref in enumerate(refs):
        kv[member ^ distance] = ref[...]


def forward_kernel(
    micro, lens_ref, place_ref, q_ref, kv_0, kv_1, kv_2, kv_3, out_ref, lse_ref, kv, acc, top, total
):
    rows = q_ref.shape[0]
    member = place_ref[0]
    places, begins, lowest = row_range(lens_ref, micro, member * rows, rows)
    place_kv(member, (kv_0, kv_1, kv_2, kv_3), kv)
    queries = [stacked(q_ref[...], g) for g in range(KV_HEADS)]
    acc[...] = jnp.zeros_like(acc)
    top[...] = jnp.full_like(top, MASKED)
    total[...] = jnp.zeros_like(total)

    def block(number, carry):
        bias = mask_of(number, rows, places, begins)
        both = kv[number]
        for g in range(KV_HEADS):
            keys, values = head_of(both, g), head_of(both, KV_HEADS + g)
            scores = dot_nt(keys, queries[g]) + bias
            before = top[g]
            now = jnp.maximum(before, jnp.max(scores, axis=0, keepdims=True))
            shrink = jnp.exp(before - now)
            weights = jnp.exp(scores - now)
            total[g] = total[g] * shrink + jnp.sum(weights, axis=0, keepdims=True)
            acc[g] = acc[g] * shrink + dot_tn(values, weights.astype(BF16))
            top[g] = now
        return carry

    lax.fori_loop(lowest // rows, member + 1, block, 0)
    done = []
    for g in range(KV_HEADS):
        done.append((acc[g] * (1.0 / total[g])).T)
        lse_ref[g] = top[g] + jnp.log(total[g])
    out_ref[...] = unstacked(done)


def backward_kernel(
    micro,
    lens_ref,
    place_ref,
    q_ref,
    kv_0,
    kv_1,
    kv_2,
    kv_3,
    out_ref,
    grad_ref,
    lse_ref,
    dq_ref,
    own_ref,
    far_ref,
    send_ref,
    kv,
    dkv,
    acc,
):
    rows = q_ref.shape[0]
    member = place_ref[0]
    places, begins, lowest = row_range(lens_ref, micro, member * rows, rows)
    place_kv(member, (kv_0, kv_1, kv_2, kv_3), kv)
    queries = [stacked(q_ref[...], g) for g in range(KV_HEADS)]
    grads = [stacked(grad_ref[...], g) for g in range(KV_HEADS)]
    product = grad_ref[...].astype(F32) * out_ref[...]
    dots = [jnp.sum(stacked(product, g).T, axis=0, keepdims=True) for g in range(KV_HEADS)]
    acc[...] = jnp.zeros_like(acc)
    dkv[...] = jnp.zeros_like(dkv)

    def block(number, carry):
        bias = mask_of(number, rows, places, begins)
        both = kv[number]
        grad_keys, grad_values = [], []
        for g in range(KV_HEADS):
            keys, values = head_of(both, g), head_of(both, KV_HEADS + g)
            probs = jnp.exp(dot_nt(keys, queries[g]) + bias - lse_ref[g])
            grad_probs = dot_nt(values, grads[g])
            grad_scores = (probs * (grad_probs - dots[g])).astype(BF16)
            grad_values.append(dot(probs.astype(BF16), grads[g]))
            grad_keys.append(dot(grad_scores, queries[g]))
            acc[g] = acc[g] + dot_tn(keys, grad_scores)
        dkv[number ^ member] = jnp.concatenate(grad_keys + grad_values, axis=1).astype(BF16)
        return carry

    lax.fori_loop(lowest // rows, member, block, 0)
    for first in range(0, rows, 128):
        start = member * rows + first
        bias = diagonal_mask(start, (first, first + 128), rows, places, begins)
        both = kv_0[first : first + 128]
        grad_keys, grad_values = [], []
        for g in range(KV_HEADS):
            keys, values = head_of(both, g), head_of(both, KV_HEADS + g)
            query, grad = rows_from(queries[g], first, rows), rows_from(grads[g], first, rows)
            shift = bias - lanes_from(lse_ref[g], first, rows)
            probs = jnp.exp(dot_nt(keys, query) + shift)
            grad_probs = dot_nt(values, grad) - lanes_from(dots[g], first, rows)
            grad_scores = (probs * grad_probs).astype(BF16)
            grad_values.append(dot(probs.astype(BF16), grad))
            grad_keys.append(dot(grad_scores, query))
            made = lanes_from(acc[g], first, rows) + dot_tn(keys, grad_scores)
            put_lanes(acc, g, made, first, rows)
        made = jnp.concatenate(grad_keys + grad_values, axis=1)
        own_ref[first : first + 128, :] = made.astype(BF16)
    dq_ref[...] = unstacked([acc[g].T for g in range(KV_HEADS)]) * HEAD_DIM**-0.5
    far_ref[...] = dkv[2]
    send_ref[0] = dkv[1]
    send_ref[1] = dkv[3]


def mid_kernel(
    members,
    parts,
    as_blocks,
    place_ref,
    x_ref,
    att_0,
    att_1,
    att_2,
    dy_ref,
    wo_ref,
    gate_ref,
    up_ref,
    down_ref,
    gain_ref,
    mixed_ref,
    dmid_ref,
    datt_ref,
    ggain_ref,
    *refs,
):
    grad_refs, held = refs[: len(refs) - 7], refs[len(refs) - 7 :]
    s_hidden, s_dgate, s_dup, s_branch, s_normed, s_dy, s_att = held
    step = pl.program_id(0)
    rows = x_ref.shape[0]
    here = pl.ds(pl.multiple_of(step * rows, rows), rows)
    gain = gain_ref[...]
    for n, ref in enumerate((att_0, att_1, att_2)):

        @pl.when(step == n)
        def _(ref=ref):
            s_att[here, :] = ref[...].astype(BF16)

    att = s_att[here, :]
    middle = x_ref[...].astype(F32) + dot(att, wo_ref[...])
    scale = norm_scale(middle)
    normed = (middle * scale * gain).astype(BF16)
    dy = dy_ref[...]
    out, dnormed = middle, 0.0
    for first in range(0, FF, FF // 2):
        cols = slice(first, first + FF // 2)
        gate = dot(normed, gate_ref[:, cols])
        up = dot(normed, up_ref[:, cols])
        sig = lax.logistic(gate)
        silu = gate * sig
        hidden = (silu * up).astype(BF16)
        s_hidden[here, cols] = hidden
        out = out + dot_nt(hidden, down_ref[:, cols])
        dhidden = dot(dy, down_ref[:, cols])
        dgate = (dhidden * up * sig * (1.0 + gate * (1.0 - sig))).astype(BF16)
        dup = (dhidden * silu).astype(BF16)
        s_dgate[here, cols] = dgate
        s_dup[here, cols] = dup
        dnormed = dnormed + dot_nt(dgate, gate_ref[:, cols]) + dot_nt(dup, up_ref[:, cols])
    mixed_ref[0] = out.T.astype(BF16)
    back, term = norm_back(middle, scale, gain, dnormed)
    dmid = dy.astype(F32) + back
    dmid_ref[...] = dmid
    branch = dmid.astype(BF16)
    datt_ref[...] = dot_nt(branch, wo_ref[...]).astype(BF16)
    s_branch[here, :] = branch
    s_normed[here, :] = normed
    s_dy[here, :] = dy

    @pl.when(step == 0)
    def _():
        ggain_ref[...] = term

    @pl.when(step > 0)
    def _():
        ggain_ref[...] += term

    @pl.when(step == pl.num_programs(0) - 1)
    def _():
        width = s_normed.shape[1]
        grad_out = dot_tn(s_att[...], s_branch[...])
        normed_t = s_normed[...].T
        dy_t = s_dy[...].T
        if not as_blocks:
            (full_ref,) = grad_refs
            full_ref[:, :FF] = dot(normed_t, s_dgate[...]).astype(BF16)
            full_ref[:, FF : 2 * FF] = dot(normed_t, s_dup[...]).astype(BF16)
            full_ref[:, 2 * FF : 3 * FF] = dot(dy_t, s_hidden[...]).astype(BF16)
            full_ref[:, 3 * FF :] = grad_out.astype(BF16)
            return
        a_keep, a_send, b_keep, b_send = grad_refs
        member, place = place_ref[0], place_ref[1]
        part = width // parts
        lanes = FF // members
        deep = FF // parts
        cols = width // members
        cut = a_keep.shape[3] - lanes
        for f in range(members):
            core, y = (member ^ f) & 1, (member ^ f) >> 1
            grad_gate = dot(normed_t, s_dgate[:, f * lanes : (f + 1) * lanes])
            grad_up = dot(normed_t, s_dup[:, f * lanes : (f + 1) * lanes])
            grad_down = dot(dy_t[f * cols : (f + 1) * cols], s_hidden[...])
            first, rest = [], []
            for n in range(parts):
                here = slice(n * part, (n + 1) * part)
                span = grad_down[:, n * deep : (n + 1) * deep]
                span = [span[i * part : (i + 1) * part] for i in range(cols // part)]
                span = [grad_up[here, cut:]] + span + [grad_out[here, f * cols : (f + 1) * cols]]
                pair = jnp.concatenate([grad_gate[here], grad_up[here, :cut]], axis=1)
                first.append(pair.astype(BF16))
                rest.append(jnp.concatenate(span, axis=1).astype(BF16))
            for side, a_ref, b_ref in ((0, a_keep, b_keep), (1, a_send, b_send)):

                @pl.when(core == side)
                def _(a_ref=a_ref, b_ref=b_ref, first=first, rest=rest, y=y):
                    for n in range(parts):
                        x, z = (place ^ n) & 1, (place ^ n) >> 1
                        a_ref[y, 4 * x + z] = first[n]
                        b_ref[x, 4 * y + z] = rest[n]


def blocks_of_rest(full, members, parts):
    width = full.shape[0]
    part, lanes, deep = width // parts, FF // members, FF // parts
    cols = width // members

    def across(first, last):
        piece = full[:, first:last].reshape(parts, part, members, (last - first) // members)
        return piece.transpose(0, 2, 1, 3)

    down = full[:, 2 * FF : 3 * FF].reshape(members, cols // part, part, parts, deep)
    down = down.transpose(3, 0, 2, 1, 4).reshape(parts, members, part, lanes)
    made = [across(0, FF), across(FF, 2 * FF), down, across(3 * FF, full.shape[1])]
    made = jnp.concatenate(made, axis=3)
    return made.reshape(parts * members, part, made.shape[3])


def post_kernel(
    x_ref,
    dq_ref,
    own_ref,
    near_ref,
    far_ref,
    dmid_ref,
    w_ref,
    gain_ref,
    cos_ref,
    sin_ref,
    *refs,
):
    dx_ref, raw_ref, normed_ref, term_ref = refs[len(refs) - 4 :]
    gain = gain_ref[...]
    x = x_ref[...].astype(F32)
    scale = norm_scale(x)
    normed_ref[...] = (x * scale * gain).astype(BF16)
    dkv = add(own_ref[...], near_ref[0]) + far_ref[...].astype(F32)
    turned = jnp.concatenate([dq_ref[...], dkv[:, :KW]], axis=1)
    turned = turn(turned, cos_ref[...], -sin_ref[...])
    raw = jnp.concatenate([turned, dkv[:, KW:]], axis=1).astype(BF16)
    raw_ref[...] = raw
    back, term = norm_back(x, scale, gain, dot_nt(raw, w_ref[...]))
    dx_ref[0] = (dmid_ref[...] + back).T
    term_ref[...] = term


def attention_blocks(grad_qkv, gain_one, gain_two, members, parts, store):
    width = grad_qkv.shape[0]
    part = width // parts
    q_cols, k_cols = QW // members, KW // members
    used = q_cols + 2 * k_cols
    lanes = padded_lanes(used)
    spare = jnp.zeros((part, lanes - used), F32)
    for n in range(parts):
        rows = slice(n * part, (n + 1) * part)
        gains = gain_lines(gain_one[:, rows], gain_two[:, rows], part, lanes)
        for f in range(members):
            spans = [
                grad_qkv[rows, f * q_cols : (f + 1) * q_cols],
                grad_qkv[rows, QW + f * k_cols : QW + (f + 1) * k_cols],
                grad_qkv[rows, QW + KW + f * k_cols : QW + KW + (f + 1) * k_cols],
                spare,
            ]
            body = jnp.concatenate(spans, axis=1)
            store(n, f, jnp.concatenate([body, gains], axis=0).astype(BF16))


def grads_kernel(members, parts, *refs):
    place_ref, raws, normeds, terms = refs[0], refs[1:4], refs[4:7], refs[7:10]
    gain_two_ref, outs = refs[10], refs[11:]
    raw = jnp.concatenate([r[...] for r in raws], axis=0)
    normed = jnp.concatenate([r[...] for r in normeds], axis=0)
    grad_qkv = dot_tn(normed, raw)
    gain_one = terms[0][...] + terms[1][...] + terms[2][...]
    if len(outs) == 2:
        outs[0][...] = grad_qkv
        outs[1][...] = gain_one
        return
    a_keep, a_send, b_keep, b_send, s_a, s_b = outs
    member, place = place_ref[0], place_ref[1]
    half = s_a.shape[4]

    def store(n, f, block):
        away = place ^ n
        x, z = away & 1, away >> 1
        away = member ^ f
        core, y = away & 1, away >> 1
        s_a[core, y, 4 * x + z] = block[:, :half]
        s_b[core, x, 4 * y + z] = block[:, half:]

    attention_blocks(grad_qkv, gain_one, gain_two_ref[...], members, parts, store)
    a_keep[...] = s_a[0]
    a_send[...] = s_a[1]
    b_keep[...] = s_b[0]
    b_send[...] = s_b[1]


def local(
    tokens,
    cotangent,
    lengths,
    gain_attn,
    w_query,
    w_key,
    w_value,
    w_out,
    gain_mlp,
    w_gate,
    w_up,
    w_down,
):
    members = lax.axis_size("fsdp")
    parts = lax.axis_size("dp")
    count = parts * members
    member = lax.axis_index("fsdp")
    micro, rows, width = tokens.shape
    every = micro * rows
    part = w_query.shape[0]
    q_cols, k_cols = w_query.shape[1], w_key.shape[1]
    lanes = w_gate.shape[1]
    deep = padded_rows(part)
    attn_lanes = padded_lanes(q_cols + 2 * k_cols)
    rest_lanes = 3 * lanes + w_out.shape[1]
    as_blocks = parts == 8 and part % 8 == 0 and width // members == 2 * part

    lens = lengths[:, 0, :]
    place = jnp.stack([member, lax.axis_index("dp")]).astype(jnp.int32)
    ends = jnp.cumsum(lens, axis=1)
    at = member * rows + lax.broadcasted_iota(jnp.int32, (micro, rows), 1)
    begins = jnp.zeros_like(at)
    for n in range(lens.shape[1]):
        following = ends[:, n : n + 1] if n < lens.shape[1] - 1 else at
        begins = jnp.where(ends[:, n : n + 1] <= at, following, begins)
    posit = (at - begins).reshape(every, 1).astype(F32)
    lane = lax.broadcasted_iota(jnp.int32, (1, 128), 1)
    halfway = HEAD_DIM // 2
    freqs = jnp.exp((lane % halfway).astype(F32) * (-math.log(ROPE_BASE) / halfway))
    angles = posit * freqs
    cosine = jnp.cos(angles)
    sine = jnp.sin(angles) * jnp.where(lane % HEAD_DIM < halfway, -1.0, 1.0)

    gain_rows = (gain_attn.reshape(1, part), gain_mlp.reshape(1, part))
    own = (w_query, w_key.T, w_value.T) + gain_rows
    others = (w_gate, w_up, w_down.T, w_out)
    if as_blocks:
        attn_block, rest_block = pl.pallas_call(
            pack_kernel,
            out_shape=(
                shape_of((deep, attn_lanes), BF16),
                shape_of((part, rest_lanes), BF16),
            ),
            in_specs=whole(9),
            out_specs=whole(2),
            compiler_params=params(56),
            cost_estimate=cost(1, 500),
            name="pack",
        )(*own, *others)
    else:
        attn_block, rest_block = pack_attention(*own), pack_rest(*others)
    rest_all = lax.all_gather(rest_block, BOTH, axis=0, tiled=False)
    smem = pl.BlockSpec(memory_space=pltpu.SMEM)
    x = tokens.reshape(every, width)
    dy = cotangent.reshape(every, width)
    if as_blocks:
        gathered, early = gather_attention(attn_block, (cosine, sine, x))
        cosine, sine, x = early
        wqkv, gain_one, gain_two = pl.pallas_call(
            functools.partial(join_attention_kernel, members, part, q_cols, k_cols),
            out_shape=(
                shape_of((width, QW + 2 * KW), BF16),
                shape_of((1, width), F32),
                shape_of((1, width), F32),
            ),
            in_specs=[smem] + whole(8),
            out_specs=whole(3),
            scratch_shapes=[pltpu.VMEM((count, deep, attn_lanes), BF16)],
            compiler_params=params(56),
            cost_estimate=cost(10, 6000),
            name="join_attention",
        )(place, *gathered)
        gate_w, up_w, down_w, wo = pl.pallas_call(
            functools.partial(join_rest_kernel, members, lanes),
            out_shape=(shape_of((width, FF), BF16),) * 3 + (shape_of((QW, width), BF16),),
            in_specs=whole(1),
            out_specs=whole(4),
            compiler_params=params(),
            cost_estimate=cost(10, 14000),
            name="join_rest",
        )(rest_all)
    else:
        attn_all = lax.all_gather(attn_block, BOTH, axis=0, tiled=False)
        wqkv, gain_one, gain_two = join_attention_plain(members, part, q_cols, k_cols, attn_all)
        gate_w, up_w, down_w, wo = join_rest_plain(members, lanes, rest_all)

    def by_rows(cols):
        return pl.BlockSpec((rows, cols), lambda n: (n, 0))

    def same(*shape):
        return pl.BlockSpec(shape, lambda n: (0,) * len(shape))

    def once(*shape):
        return pl.BlockSpec(
            shape, lambda n: (0,) * len(shape), pipeline_mode=pl.Buffered(buffer_count=1)
        )

    def only(number, cols):
        return pl.BlockSpec((rows, cols), lambda n: (number, 0))

    def turned(number):
        return pl.BlockSpec((1, width, rows), lambda n: (number, 0, 0))

    held = pltpu.VMEM((KV_HEADS, HEAD_DIM, REPEATS * rows), F32)
    line = (KV_HEADS, 1, REPEATS * rows)
    kv_blocks = pltpu.VMEM((members, rows, 2 * KW), BF16)
    kv_block = same(rows, 2 * KW)
    outward = [(0, 2), (1, 3)]
    queries, sent = [], []
    for m in range(micro):
        query, kv = pl.pallas_call(
            pre_kernel,
            grid=(1,),
            out_shape=(shape_of((rows, QW), BF16), shape_of((rows, 2 * KW), BF16)),
            in_specs=[
                only(m, width),
                same(width, QW + 2 * KW),
                same(1, width),
                only(m, 128),
                only(m, 128),
            ],
            out_specs=(same(rows, QW), same(rows, 2 * KW)),
            compiler_params=params(),
            cost_estimate=cost(500, 6000),
            name="pre",
        )(x, wqkv, gain_one, cosine, sine)
        queries.append(query)
        sent.append((kv, swap(kv, "fsdp", 1), lax.ppermute(kv, "fsdp", outward)))

    kvs, attended, logsums = [], [], []
    for m in range(micro):
        far = after(sent[m][2], *attended[-1:])
        kvs.append(sent[m][:2] + (far, swap(far, "fsdp", 1)))
        out, logsum = pl.pallas_call(
            functools.partial(forward_kernel, m),
            grid=(1,),
            out_shape=(shape_of((rows, QW), F32), shape_of(line, F32)),
            in_specs=[smem, smem, same(rows, QW)] + [kv_block] * 4,
            out_specs=(same(rows, QW), same(*line)),
            scratch_shapes=[kv_blocks, held, pltpu.VMEM(line, F32), pltpu.VMEM(line, F32)],
            compiler_params=params(),
            cost_estimate=cost(8000, 4000),
            name="attend_forward",
        )(lens, place, queries[m], *kvs[m])
        attended.append(out)
        logsums.append(logsum)

    if as_blocks:
        cut = rest_lanes // 256 * 128
        halves = (cut, cut, rest_lanes - cut, rest_lanes - cut)
        grad_shapes = [(2, 8, part, lane_count) for lane_count in halves]
    else:
        grad_shapes = [(width, 3 * FF + width)]
    mixed, dmid, datt, grad_two, *grad_rest = pl.pallas_call(
        functools.partial(mid_kernel, members, parts, as_blocks),
        grid=(micro,),
        out_shape=[
            shape_of((micro, width, rows), BF16),
            shape_of((every, width), F32),
            shape_of((every, QW), BF16),
            shape_of((1, width), F32),
        ]
        + [shape_of(s, BF16) for s in grad_shapes],
        in_specs=[smem, by_rows(width)]
        + [once(rows, QW)] * 3
        + [
            by_rows(width),
            once(QW, width),
            once(width, FF),
            once(width, FF),
            once(width, FF),
            once(1, width),
        ],
        out_specs=[
            pl.BlockSpec((1, width, rows), lambda n: (n, 0, 0)),
            by_rows(width),
            by_rows(QW),
            same(1, width),
        ]
        + [once(*s) for s in grad_shapes],
        scratch_shapes=[
            pltpu.VMEM((every, FF), BF16),
            pltpu.VMEM((every, FF), BF16),
            pltpu.VMEM((every, FF), BF16),
            pltpu.VMEM((every, width), BF16),
            pltpu.VMEM((every, width), BF16),
            pltpu.VMEM((every, width), BF16),
            pltpu.VMEM((every, QW), BF16),
        ],
        compiler_params=params(60),
        cost_estimate=cost(40000, 40000),
        name="mid",
    )(place, x, *attended, dy, wo, gate_w, up_w, down_w, gain_two)

    if as_blocks:
        steps = reduce_steps(*grad_rest)
        got = next(steps)[1]
    else:
        grad_rest = blocks_of_rest(grad_rest[0], members, parts)
        rest_sum = lax.psum_scatter(grad_rest, BOTH, scatter_dimension=0, tiled=False)

    back = []
    for m in range(micro):
        query = queries[m]
        if m == 1 and as_blocks:
            send, got = steps.send([after(value, back[0][0]) for value in got])
            query = after(query, *send)
        if m == 2:
            send = ()
            if as_blocks:
                send, got = steps.send([after(value, back[1][0]) for value in got])
            query = after(query, back[0][3], *send)
        dq, keep, far, send = pl.pallas_call(
            functools.partial(backward_kernel, m),
            grid=(1,),
            out_shape=(
                shape_of((rows, QW), F32),
                shape_of((rows, 2 * KW), BF16),
                shape_of((rows, 2 * KW), BF16),
                shape_of((2, rows, 2 * KW), BF16),
            ),
            in_specs=[smem, smem, same(rows, QW)]
            + [kv_block] * 4
            + [same(rows, QW), only(m, QW), same(*line)],
            out_specs=(same(rows, QW), kv_block, kv_block, same(2, rows, 2 * KW)),
            scratch_shapes=[kv_blocks, kv_blocks, held],
            compiler_params=params(),
            cost_estimate=cost(11000, 5000),
            name="attend_backward",
        )(lens, place, query, *kvs[m], attended[m], datt, logsums[m])
        near = swap(send, "fsdp", 1)
        far = add(far, near[1]).astype(BF16)
        back.append((dq, keep, near, far))
    inward = [(b, a) for a, b in outward]
    if as_blocks:
        send, got = steps.send([after(value, back[-1][0]) for value in got])
        back[0] = (after(back[0][0], *send),) + back[0][1:]

    input_grad = ()
    raws, normeds, terms = [], [], []
    for m in range(micro):
        dq, keep, near, far = back[m]
        far = lax.ppermute(far, "fsdp", inward)
        made, raw, normed, term = pl.pallas_call(
            post_kernel,
            grid=(1,),
            out_shape=(
                shape_of((micro, width, rows), F32),
                shape_of((rows, QW + 2 * KW), BF16),
                shape_of((rows, width), BF16),
                shape_of((1, width), F32),
            ),
            in_specs=[
                only(m, width),
                same(rows, QW),
                kv_block,
                pl.BlockSpec((1, rows, 2 * KW), lambda n: (0, 0, 0)),
                kv_block,
                only(m, width),
                same(width, QW + 2 * KW),
                same(1, width),
                only(m, 128),
                only(m, 128),
            ]
            + [pl.BlockSpec(memory_space=pl.ANY)] * len(input_grad),
            out_specs=(
                turned(m),
                same(rows, QW + 2 * KW),
                same(rows, width),
                same(1, width),
            ),
            input_output_aliases={10: 0} if input_grad else {},
            compiler_params=params(),
            cost_estimate=cost(2000, 8000),
            name="post",
        )(x, dq, keep, near, far, dmid, wqkv, gain_one, cosine, sine, *input_grad)
        input_grad = (made,)
        raws.append(raw)
        normeds.append(normed)
        terms.append(term)

    if as_blocks:
        terms[-1] = after(terms[-1], *got)
        made = (shape_of((2, 8, deep, attn_lanes // 2), BF16),) * 4
        scratch = [pltpu.VMEM((2, 2, 8, deep, attn_lanes // 2), BF16)] * 2
    else:
        made = (shape_of((width, QW + 2 * KW), F32), shape_of((1, width), F32))
        scratch = []
    made = pl.pallas_call(
        functools.partial(grads_kernel, members, parts),
        out_shape=made,
        in_specs=[smem] + whole(10),
        out_specs=whole(len(made)),
        scratch_shapes=scratch,
        compiler_params=params(),
        cost_estimate=cost(3000, 8000),
        name="grads",
    )(place, *raws, *normeds, *terms, grad_two)

    if as_blocks:
        rest_sum = steps.send(got)
        shapes = [
            (part, q_cols),
            (k_cols, part),
            (k_cols, part),
            (1, part),
            (1, part),
            w_gate.shape,
            w_up.shape,
            w_down.shape[::-1],
            w_out.shape,
        ]
        grads = pl.pallas_call(
            unpack_kernel,
            out_shape=tuple(shape_of(s, F32) for s in shapes),
            in_specs=whole(8),
            out_specs=whole(9),
            compiler_params=params(),
            cost_estimate=cost(1, 3000),
            name="unpack",
        )(*reduce_all(made), *rest_sum)
    else:
        blocks = []
        attention_blocks(
            made[0], made[1], grad_two, members, parts, lambda n, f, block: blocks.append(block)
        )
        attn_sum = lax.psum_scatter(
            jnp.stack(blocks), BOTH, scatter_dimension=0, tiled=False
        ).astype(F32)
        grads = unpack_attention(attn_sum, part, q_cols, k_cols)
        grads += unpack_rest(rest_sum, lanes, w_down.shape[::-1])
    g_query, g_key, g_value, g_one, g_two, g_gate, g_up, g_down, g_out = grads
    return (
        mixed.transpose(0, 2, 1),
        input_grad[0].transpose(0, 2, 1),
        g_one.reshape(-1),
        g_query,
        g_key.T,
        g_value.T,
        g_out,
        g_two.reshape(-1),
        g_gate,
        g_up,
        g_down.T,
    )


def solution(mesh):
    rows = P(None, BOTH, None)
    block = P(*BOTH)
    gain = P("dp")
    in_specs = (rows, rows, P(None, "dp", None), gain)
    in_specs += (block, block, block, block, gain, block, block, block)
    out_specs = (rows, rows, gain, block, block, block, block, gain, block, block, block)
    return jax.shard_map(local, mesh=mesh, in_specs=in_specs, out_specs=out_specs, check_vma=False)
```
